256 devices in a mesh: tok: 64 (over y, z, core), head: 4 (over x).
Axes of the slice: x: 4, y: 4, z: 8, core: 2. Of those that a mesh axis runs over, the one named last changes fastest.
Arguments:
- queries: bfloat16 [2, 16384, 16, 256], P(None, 'tok', 'head'), may hold values from -6 to 6
- key_input: bfloat16 [2, 16384, 16, 256], P(None, 'tok', 'head'), may hold values from -6 to 6
- value_input: bfloat16 [2, 16384, 16, 256], P(None, 'tok', 'head'), may hold values from -6 to 6
- token_rates: float32 [2, 16, 16384], P(None, 'head', 'tok'), may hold values from 0.05 to 1
- fast_weights: float32 [16, 3, 256, 256], P('head'), may hold values from -0.375 to 0.375
- update_rate: float32 [16, 3], P('head'), may hold values from 0.2 to 1
- out_gain: float32 [16, 256], P('head'), may hold values from 0.5 to 1.5
Outputs:
- transformed: bfloat16 [2, 16384, 16, 256], P(None, 'tok', 'head')
The draws below stay inside these ranges and needn't reach their ends.
All inputs are finite; a program needn't handle non-finite values.
Results may differ from the reference program's by a relative error of at most 0.029.
Values may be sent and summed in bfloat16 or wider, within the bound.
A program may use at most 64 MiB of HBM per device.

```python
import math
import jax
import jax.numpy as jnp
from jax import lax

DH = 256
HEADS = 16
TOKENS = 16384
BLOCKS = 2
NS_STEPS = 3


def levels(stream_key, shape, cuts, least, high):
    factor_of = 1.0
    for axis_at, shards_of in cuts:
        draws = jax.random.uniform(jax.random.fold_in(jax.random.fold_in(stream_key, 6), axis_at), (shards_of,), jnp.float32, least / len(cuts), high / len(cuts))
        factor_of = factor_of * jnp.repeat(jnp.exp(draws), shape[axis_at] // shards_of).reshape((-1,) + (1,) * (len(shape) - 1 - axis_at))
    return factor_of


def normal_values(rng, shape, spread, most, cuts=(), kind=jnp.bfloat16):
    drawn = jax.random.normal(rng, shape, jnp.float32) * spread
    if len(cuts) > 0:
        drawn = levels(rng, shape, cuts, -0.22, 0.18) * drawn
    return jnp.clip(drawn, min=-most, max=most).astype(kind)


def setup_inputs(seed: int = 0) -> dict:
    seeds = jax.random.split(jax.random.key(seed), 8)
    return {
        "queries": normal_values(seeds[0], (BLOCKS, TOKENS, HEADS, DH), 1.0, 6.0, ((1, 64), (2, 4))),
        "key_input": normal_values(seeds[1], (BLOCKS, TOKENS, HEADS, DH), 1.0, 6.0, ((1, 64), (2, 4))),
        "value_input": normal_values(seeds[2], (BLOCKS, TOKENS, HEADS, DH), 1.0, 6.0, ((1, 64), (2, 4))),
        "token_rates": jnp.clip(jnp.exp(math.log(1.0) - 2.9957323 * jax.random.uniform(seeds[3], (BLOCKS, HEADS, TOKENS), jnp.float32) ** levels(seeds[3], (BLOCKS, HEADS, TOKENS), ((1, 4), (2, 64)), -0.2, 0.2)), 0.05, 1.0),
        "fast_weights": normal_values(seeds[4], (HEADS, 3, DH, DH), DH ** -0.5, 0.375, ((0, 4),), jnp.float32),
        "update_rate": jnp.clip(0.2 + 0.8 * jax.random.uniform(seeds[5], (HEADS, 3), jnp.float32) ** levels(seeds[5], (HEADS, 3), ((0, 4),), -0.2, 0.2), 0.2, 1.0),
        "out_gain": jnp.clip(1.0 + 0.1 * jax.random.normal(seeds[6], (HEADS, DH), jnp.float32), 0.5, 1.5),
    }


coef_a = 3.4445
coef_b = -4.775
coef_c = 2.0315

def head_grads(key_rows, value_rows, rate_rows, weights):
    w_bf = weights.astype(jnp.bfloat16)
    gate_pre = jnp.dot(key_rows, w_bf[0], preferred_element_type=jnp.float32)
    up_pre = jnp.dot(key_rows, w_bf[2], preferred_element_type=jnp.float32)
    sigmoid_gate = jax.nn.sigmoid(gate_pre)
    activated = gate_pre * sigmoid_gate
    hidden = (activated * up_pre).astype(jnp.bfloat16)
    target = (-rate_rows[:, None] * value_rows.astype(jnp.float32)).astype(jnp.bfloat16)
    grad_down = jnp.dot(hidden.T, target, preferred_element_type=jnp.float32)
    back_prop = jnp.dot(target, w_bf[1].T, preferred_element_type=jnp.float32)
    up_cot = (back_prop * activated).astype(jnp.bfloat16)
    gate_cot = (back_prop * up_pre * sigmoid_gate * (1.0 + gate_pre * (1.0 - sigmoid_gate))).astype(jnp.bfloat16)
    grad_gate = jnp.dot(key_rows.T, gate_cot, preferred_element_type=jnp.float32)
    grad_up = jnp.dot(key_rows.T, up_cot, preferred_element_type=jnp.float32)
    return jnp.stack([grad_gate, grad_down, grad_up])

def orthogonalize(grad_mat):
    inverse = lax.rsqrt(jnp.sum(grad_mat * grad_mat) + 1e-06)
    iterate = lax.optimization_barrier((grad_mat * inverse).astype(jnp.bfloat16))
    for step_idx in range(NS_STEPS):
        gram = lax.optimization_barrier(jnp.dot(iterate, iterate.T, preferred_element_type=jnp.float32).astype(jnp.bfloat16))
        poly = (coef_b * gram.astype(jnp.float32) + coef_c * jnp.dot(gram, gram, preferred_element_type=jnp.float32)).astype(jnp.bfloat16)
        iterate = lax.optimization_barrier((coef_a * iterate.astype(jnp.float32) + jnp.dot(poly, iterate, preferred_element_type=jnp.float32)).astype(jnp.bfloat16))
    return iterate

def apply_head(query_rows, w_bf):
    gate_pre = jnp.dot(query_rows, w_bf[0], preferred_element_type=jnp.float32)
    up_pre = jnp.dot(query_rows, w_bf[2], preferred_element_type=jnp.float32)
    hidden = (gate_pre * jax.nn.sigmoid(gate_pre) * up_pre).astype(jnp.bfloat16)
    return jnp.dot(hidden, w_bf[1], preferred_element_type=jnp.float32)

def reference(queries, key_input, value_input, token_rates, fast_weights, update_rate, out_gain):
    weights = fast_weights
    results = []
    for block_idx in range(BLOCKS):
        key_heads = jnp.swapaxes(key_input[block_idx], 0, 1)
        value_heads = jnp.swapaxes(value_input[block_idx], 0, 1)
        grads = lax.map(lambda packed: head_grads(*packed), (key_heads, value_heads, token_rates[block_idx], weights))
        ortho = lax.map(orthogonalize, grads.reshape(HEADS * 3, DH, DH)).reshape(HEADS, 3, DH, DH)
        weights = weights - update_rate[:, :, None, None] * ortho.astype(jnp.float32)
        w_bf = weights.astype(jnp.bfloat16)
        query_heads = jnp.swapaxes(queries[block_idx], 0, 1)
        mapped = lax.map(lambda packed: apply_head(*packed), (query_heads, w_bf))
        squares = lax.optimization_barrier(jnp.sum(mapped * mapped, axis=(0, 2)))
        scale_rows = lax.rsqrt(squares / (HEADS * DH) + 1e-06)
        normed = mapped * scale_rows[None, :, None] * out_gain[:, None, :]
        results.append(jnp.swapaxes(normed, 0, 1).astype(jnp.bfloat16))
    return jnp.stack(results)
```

```python
import functools

import jax
import jax.numpy as jnp
from jax import lax
from jax.experimental import pallas as pl
from jax.experimental.pallas import tpu as pltpu
from jax.sharding import PartitionSpec as P

NS_STEPS = 3
SIZE_Y = 4

coef_a = 3.4445
coef_b = -4.775
coef_c = 2.0315

BF = jnp.bfloat16
F32 = jnp.float32
MESH = pl.DeviceIdType.MESH
KEY, TGT, QRY = 0, 1, 2

ROUTES = (
    (0, 1, 1, 0, 128, 256),
    (0, -1, 1, 128, 128, 384),
    (1, 0, 2, 0, 128, 512),
    (-1, 0, 2, 128, 128, 640),
    (1, 1, 3, 0, 64, 768),
    (1, -1, 3, 64, 64, 832),
    (-1, 1, 3, 128, 64, 896),
    (-1, -1, 3, 192, 64, 960),
)


def mm(a, b):
    return jnp.dot(a, b, preferred_element_type=F32)


def mm_nt(a, b):
    return lax.dot_general(a, b, (((1,), (1,)), ((), ())), preferred_element_type=F32)


def mm_tn(a, b):
    return lax.dot_general(a, b, (((0,), (0,)), ((), ())), preferred_element_type=F32)


def kernel(
    size_z, size_x,
    q_hbm, k_hbm, v_hbm, rate_ref, w_hbm, lr_ref, gain_ref, out_hbm,
    raw, raw_out, moved, staged, weights, weights_bf, hid, gate_cot, up_cot, grads,
    pair_src, pair_dst, half, ring_src, ring_dst, full, map_src, map_dst, tile_buf, sq_src, sq_dst,
    load_sem, w_sem, store_sem, move_s, move_r, pair_s, pair_r, ring_s, ring_r, all_s, all_r,
    twin_s, twin_r, back_s, back_r, sq_s, sq_r,
):
    bits_z = size_z.bit_length() - 1
    half_y, half_z = SIZE_Y // 2, size_z // 2
    members = half_y * half_z
    piece = 128 // members
    total_heads = 4 * size_x
    tok = lax.axis_index("tok")
    head_x = lax.axis_index("head")
    core = tok & 1
    z = (tok >> 1) & (size_z - 1)
    y = tok >> (1 + bits_z)
    own = 2 * (y & 1) + (z & 1)
    group = (y >> 1) * half_z + (z >> 1)

    def chip(dy, dz, dc=0):
        at_y = (y + dy) & (SIZE_Y - 1)
        at_z = (z + dz) & (size_z - 1)
        return {"tok": (at_y * size_z + at_z) * 2 + (core ^ dc)}

    def across(step):
        return {"head": (head_x + step) & (size_x - 1)}

    peers = [(i, j) for i in range(half_y) for j in range(half_z) if i + j > 0]

    sources = {KEY: k_hbm, TGT: v_hbm, QRY: q_hbm}

    def load(kind, b):
        return pltpu.make_async_copy(sources[kind].at[b], raw.at[kind, b], load_sem.at[kind, b])

    load(KEY, 0).start()
    load(TGT, 0).start()
    w_load = pltpu.make_async_copy(w_hbm.at[own], weights, w_sem)
    w_load.start()
    for kind, b in ((KEY, 1), (TGT, 1), (QRY, 0), (QRY, 1)):
        load(kind, b).start()

    barrier = pltpu.get_barrier_semaphore()
    greeted = [chip(dy, dz) for dy, dz, *_ in ROUTES]
    greeted += [chip(2 * i, 2 * j) for i, j in peers]
    greeted += [chip(0, 0, 1)]
    greeted += [across(s) for s in range(1, size_x)]
    for device in greeted:
        pl.semaphore_signal(barrier, inc=1, device_id=device, device_id_type=MESH)

    rows_i = lax.broadcasted_iota(jnp.int32, (256, 256), 0)
    cols_i = lax.broadcasted_iota(jnp.int32, (256, 256), 1)

    def source_row(i):
        return (i & 31) * 8 + ((i >> 5) & 1) * 4 + ((i >> 6) ^ own)

    gather = jnp.where(source_row(rows_i) == cols_i, 1.0, 0.0).astype(BF)
    scatter = jnp.where(source_row(cols_i) == rows_i, 1.0, 0.0).astype(BF)

    def split_heads(kind, b):
        load(kind, b).wait()
        if kind == TGT:
            rates = []
            for r in range(4):
                row = rate_ref[b, pl.ds(r ^ own, 1), :]
                rates.append(-jnp.transpose(jnp.broadcast_to(row, (128, 256))))
        for g in range(4):
            lo = raw[kind, b, 512 * g : 512 * g + 256, :]
            hi = raw[kind, b, 512 * g + 256 : 512 * g + 512, :]
            out = mm(gather, jnp.concatenate([lo, hi], axis=1))
            for r in range(4):
                for c in range(2):
                    for k in range(2):
                        t = 64 * g + 32 * k
                        tile = out[64 * r + 32 * c : 64 * r + 32 * c + 32, 128 * k : 128 * k + 128]
                        if kind == TGT:
                            tile = tile * rates[r][t : t + 32, :]
                        tile = tile.astype(BF)
                        cols = slice(128 * c, 128 * c + 128)
                        if r == 0:
                            moved[b, kind, t : t + 32, cols] = tile
                        else:
                            staged[b, kind, r - 1, t : t + 32, cols] = tile

    def remote(src, dst, s, r, device):
        return pltpu.make_async_remote_copy(
            src_ref=src, dst_ref=dst, send_sem=s, recv_sem=r, device_id=device, device_id_type=MESH
        )

    def send_moved(kind, b):
        for dy, dz, r, t, n, row in ROUTES:
            remote(
                staged.at[b, kind, r - 1, pl.ds(t, n)],
                moved.at[b, kind, pl.ds(row, n)],
                move_s.at[b, kind], move_r.at[b, kind], chip(dy, dz),
            ).start()

    def moved_all(kind, b):
        return remote(
            staged.at[b, kind], staged.at[b, kind], move_s.at[b, kind], move_r.at[b, kind], chip(0, 1)
        )

    def gradients(b):
        for i in range(4):
            rows = slice(256 * i, 256 * i + 256)
            key = moved[b, KEY, rows, :]
            gate_pre = mm(key, weights_bf[0])
            up_pre = mm(key, weights_bf[2])
            back = mm_nt(moved[b, TGT, rows, :], weights_bf[1])
            sg = jax.nn.sigmoid(gate_pre)
            act = gate_pre * sg
            hid[rows, :] = (act * up_pre).astype(BF)
            up_cot[rows, :] = (back * act).astype(BF)
            gate_cot[rows, :] = (back * up_pre * sg * (1.0 + gate_pre * (1.0 - sg))).astype(BF)
        grads[0] = mm_tn(moved[b, KEY], gate_cot[...])
        grads[1] = mm_tn(hid[...], moved[b, TGT])
        grads[2] = mm_tn(moved[b, KEY], up_cot[...])

    def pair_copy(b):
        return remote(pair_src.at[b], pair_dst.at[b], pair_s.at[b], pair_r.at[b], chip(0, 0, 1))

    def send_pair(b):
        other = pl.multiple_of((1 - core) * 128, 128)
        pair_src[b] = grads[:, pl.ds(other, 128), :].astype(BF)
        pair_copy(b).start()

    def ring_all(b):
        return remote(ring_dst.at[b], ring_dst.at[b], ring_s.at[b], ring_r.at[b], chip(0, 2))

    def send_ring(b):
        mine = pl.multiple_of(core * 128, 128)
        pair_copy(b).wait_recv()
        total = grads[:, pl.ds(mine, 128), :] + pair_dst[b].astype(F32)
        half[...] = total
        ring_src[b] = total.astype(BF)
        for k, (i, j) in enumerate(peers):
            there = (((y >> 1) + i) & (half_y - 1)) * half_z + (((z >> 1) + j) & (half_z - 1))
            rows = pl.ds(pl.multiple_of(there * piece, piece), piece)
            remote(
                ring_src.at[b, :, rows, :], ring_dst.at[b, k], ring_s.at[b], ring_r.at[b], chip(2 * i, 2 * j)
            ).start()

    def all_all(b):
        return remote(ring_dst.at[b], ring_dst.at[b], all_s.at[b], all_r.at[b], chip(0, 2))

    def send_all(b):
        ring_all(b).wait_recv()
        total = half[:, pl.ds(pl.multiple_of(group * piece, piece), piece), :]
        for k in range(len(peers)):
            total = total + ring_dst[b, k].astype(F32)
        rows = pl.ds(pl.multiple_of(core * 128 + group * piece, piece), piece)
        full[b, :, rows, :] = total.astype(BF)
        for i, j in peers:
            remote(
                full.at[b, :, rows, :], full.at[b, :, rows, :], all_s.at[b], all_r.at[b], chip(2 * i, 2 * j)
            ).start()

    def twin_copy(b):
        rows = pl.ds(pl.multiple_of(core * 128, 128), 128)
        return remote(full.at[b, :, rows, :], full.at[b, :, rows, :], twin_s.at[b], twin_r.at[b], chip(0, 0, 1))

    def send_twin(b):
        all_all(b).wait_recv()
        twin_copy(b).start()

    def update(b):
        xs, inverse = [], []
        for m in range(3):
            x = full[b, m]
            xf = x.astype(F32)
            xs.append(x)
            inverse.append(lax.rsqrt(jnp.sum(xf * xf, keepdims=True) + 1e-06))
        for step in range(NS_STEPS):
            grams = []
            for m in range(3):
                gram = mm_nt(xs[m], xs[m])
                if step == 0:
                    gram = gram * inverse[m] * inverse[m]
                grams.append(gram.astype(BF))
            polys = [
                (coef_b * grams[m].astype(F32) + coef_c * mm(grams[m], grams[m])).astype(BF) for m in range(3)
            ]
            for m in range(3):
                x = coef_a * xs[m].astype(F32) + mm(polys[m], xs[m])
                if step == 0:
                    x = x * inverse[m]
                xs[m] = x.astype(BF)
        for m in range(3):
            new = weights[m] - lr_ref[own, m] * xs[m].astype(F32)
            weights[m] = new
            weights_bf[m] = new.astype(BF)

    def apply(b):
        for i in range(4):
            rows = slice(256 * i, 256 * i + 256)
            query = moved[b, QRY, rows, :]
            gate = mm(query, weights_bf[0])
            up = mm(query, weights_bf[2])
            mapped = mm((gate * jax.nn.sigmoid(gate) * up).astype(BF), weights_bf[1]).astype(BF)
            if i == 0:
                map_dst[b, 0] = mapped
            else:
                map_src[b, i - 1] = mapped

    def send_back(b):
        for dy, dz, r, t, n, row in ROUTES:
            at = row - 256
            remote(
                map_src.at[b, at // 256, pl.ds(at % 256, n)],
                map_dst.at[b, r, pl.ds(t, n)],
                back_s.at[b], back_r.at[b], chip(-dy, -dz),
            ).start()

    def back_all(b):
        return remote(map_src.at[b], map_src.at[b], back_s.at[b], back_r.at[b], chip(0, 1))

    def squares_all(b):
        return remote(sq_dst.at[b], sq_dst.at[b], sq_s.at[b], sq_r.at[b], across(1))

    def send_squares(b):
        back_all(b).wait_recv()
        squares = jnp.zeros((256, 256), F32)
        for r in range(4):
            part = map_dst[b, r].astype(F32)
            squares = squares + part * part
        high = squares.astype(BF)
        low = (squares - high.astype(F32)).astype(BF)
        ones = jnp.ones((8, 256), BF)
        sq_src[b] = mm_nt(ones, high) + mm_nt(ones, low)
        for s in range(1, size_x):
            remote(sq_src.at[b], sq_dst.at[b, s - 1], sq_s.at[b], sq_r.at[b], across(s)).start()

    def store(b):
        return pltpu.make_async_copy(raw_out.at[b], out_hbm.at[b], store_sem.at[b])

    def finish(b):
        total = sq_src[b]
        if size_x > 1:
            squares_all(b).wait_recv()
            for s in range(1, size_x):
                total = total + sq_dst[b, s - 1]
        scale = lax.rsqrt(total * (1.0 / (total_heads * 256)) + 1e-06)
        scale = jnp.transpose(jnp.broadcast_to(scale[0:1, :], (128, 256)))
        gains = [gain_ref[pl.ds(r ^ own, 1), :] for r in range(4)]
        for g in range(4):
            for r in range(4):
                for c in range(2):
                    for k in range(2):
                        t = 64 * g + 32 * k
                        cols = slice(128 * c, 128 * c + 128)
                        tile = map_dst[b, r, t : t + 32, cols].astype(F32) * scale[t : t + 32, :]
                        tile = tile * gains[r][:, cols]
                        tile_buf[g, 64 * r + 32 * c : 64 * r + 32 * c + 32, 128 * k : 128 * k + 128] = tile.astype(BF)
        for g in range(4):
            out = mm(scatter, tile_buf[g]).astype(BF)
            raw_out[b, 512 * g : 512 * g + 256, :] = out[:, :128]
            raw_out[b, 512 * g + 256 : 512 * g + 512, :] = out[:, 128:]
        store(b).start()

    split_heads(KEY, 0)
    pl.semaphore_wait(barrier, len(greeted))
    send_moved(KEY, 0)
    split_heads(TGT, 0)
    send_moved(TGT, 0)
    w_load.wait()
    weights_bf[...] = weights[...].astype(BF)
    split_heads(KEY, 1)
    split_heads(TGT, 1)
    split_heads(QRY, 0)
    split_heads(QRY, 1)
    moved_all(KEY, 0).wait_recv()
    moved_all(TGT, 0).wait_recv()
    gradients(0)
    send_pair(0)
    send_moved(KEY, 1)
    send_moved(TGT, 1)
    send_ring(0)
    send_all(0)
    send_twin(0)
    send_moved(QRY, 0)
    send_moved(QRY, 1)
    twin_copy(0).wait_recv()
    update(0)
    moved_all(KEY, 1).wait_recv()
    moved_all(TGT, 1).wait_recv()
    gradients(1)
    send_pair(1)
    send_ring(1)
    moved_all(QRY, 0).wait_recv()
    apply(0)
    send_all(1)
    send_twin(1)
    send_back(0)
    twin_copy(1).wait_recv()
    update(1)
    moved_all(QRY, 1).wait_recv()
    apply(1)
    send_back(1)
    send_squares(0)
    finish(0)
    send_squares(1)
    finish(1)
    for b in range(2):
        for kind in (KEY, TGT, QRY):
            moved_all(kind, b).wait_send()
        pair_copy(b).wait_send()
        ring_all(b).wait_send()
        all_all(b).wait_send()
        twin_copy(b).wait_send()
        back_all(b).wait_send()
        if size_x > 1:
            squares_all(b).wait_send()
        store(b).wait()


def per_device(size_z, size_x, queries, key_input, value_input, token_rates, fast_weights, update_rate, out_gain):
    members = (SIZE_Y // 2) * (size_z // 2)
    piece = 128 // members

    def flat(a):
        return a.reshape(2, 256, 4, 2, 128).transpose(0, 1, 3, 2, 4).reshape(2, 2048, 128)

    vmem = pl.BlockSpec(memory_space=pltpu.VMEM)
    smem = pl.BlockSpec(memory_space=pltpu.SMEM)
    hbm = pl.BlockSpec(memory_space=pl.ANY)
    dma = pltpu.SemaphoreType.DMA
    out = pl.pallas_call(
        functools.partial(kernel, size_z, size_x),
        out_shape=jax.ShapeDtypeStruct((2, 2048, 128), BF),
        in_specs=[hbm, hbm, hbm, vmem, hbm, smem, vmem],
        out_specs=hbm,
        scratch_shapes=[
            pltpu.VMEM((3, 2, 2048, 128), BF),
            pltpu.VMEM((2, 2048, 128), BF),
            pltpu.VMEM((2, 3, 1024, 256), BF),
            pltpu.VMEM((2, 3, 3, 256, 256), BF),
            pltpu.VMEM((3, 256, 256), F32),
            pltpu.VMEM((3, 256, 256), BF),
            pltpu.VMEM((1024, 256), BF),
            pltpu.VMEM((1024, 256), BF),
            pltpu.VMEM((1024, 256), BF),
            pltpu.VMEM((3, 256, 256), F32),
            pltpu.VMEM((2, 3, 128, 256), BF),
            pltpu.VMEM((2, 3, 128, 256), BF),
            pltpu.VMEM((3, 128, 256), F32),
            pltpu.VMEM((2, 3, 128, 256), BF),
            pltpu.VMEM((2, members - 1, 3, piece, 256), BF),
            pltpu.VMEM((2, 3, 256, 256), BF),
            pltpu.VMEM((2, 3, 256, 256), BF),
            pltpu.VMEM((2, 4, 256, 256), BF),
            pltpu.VMEM((4, 256, 256), BF),
            pltpu.VMEM((2, 8, 256), F32),
            pltpu.VMEM((2, max(size_x - 1, 1), 8, 256), F32),
            dma((3, 2)), dma, dma((2,)),
            dma((2, 3)), dma((2, 3)),
            *[dma((2,)) for _ in range(12)],
        ],
        compiler_params=pltpu.CompilerParams(
            collective_id=0, has_side_effects=True, vmem_limit_bytes=48 * 1024 * 1024
        ),
        cost_estimate=pl.CostEstimate(flops=12_000_000_000, bytes_accessed=5_000_000, transcendentals=1_000_000),
    )(flat(queries), flat(key_input), flat(value_input), token_rates, fast_weights, update_rate, out_gain)
    return out.reshape(2, 256, 2, 4, 128).transpose(0, 1, 3, 2, 4).reshape(2, 256, 4, 256)


def solution(mesh):
    size_z = mesh.shape["tok"] // (2 * SIZE_Y)
    return jax.shard_map(
        functools.partial(per_device, size_z, mesh.shape["head"]),
        mesh=mesh,
        in_specs=(
            P(None, "tok", "head", None),
            P(None, "tok", "head", None),
            P(None, "tok", "head", None),
            P(None, "head", "tok"),
            P("head", None, None, None),
            P("head", None),
            P("head", None),
        ),
        out_specs=P(None, "tok", "head", None),
        check_vma=False,
    )
```

```python
import functools

import jax
import jax.numpy as jnp
from jax import lax
from jax.experimental import pallas as pl
from jax.experimental.pallas import tpu as pltpu
from jax.sharding import PartitionSpec as P

NS_STEPS = 3
SIZE_Y = 4

coef_a = 3.4445
coef_b = -4.775
coef_c = 2.0315

BF = jnp.bfloat16
F32 = jnp.float32
MESH = pl.DeviceIdType.MESH
KEY, TGT, QRY = 0, 1, 2
HALF = 128

ROUTES = (
    (-1, 1, 2, 0, 768),
    (1, -1, 2, 128, 896),
    (0, 1, 1, 0, 256),
    (-1, 0, 1, 128, 384),
    (0, -1, 3, 0, 512),
    (1, 0, 3, 128, 640),
)


def mm(a, b):
    return jnp.dot(a, b, preferred_element_type=F32)


def mm_nt(a, b):
    return lax.dot_general(a, b, (((1,), (1,)), ((), ())), preferred_element_type=F32)


def mm_tn(a, b):
    return lax.dot_general(a, b, (((0,), (0,)), ((), ())), preferred_element_type=F32)


def kernel(
    size_z, size_x,
    q_hbm, k_hbm, v_hbm, rate_hbm, w_hbm, lr_hbm, gain_hbm, out_hbm,
    raw, rate_ref, lr_ref, gain_ref, raw_out, moved, staged, query, query_staged,
    weights, weights_bf, w_gu, w_down, hid, cots, sums, ring_src, ring_dst, full,
    map_src, map_dst, tile_buf, row_src, row_dst, sq_src, sq_dst,
    load_sem, w_sem, small_sem, store_sem, move_s, move_r, fwd_s, fwd_r, query_s, query_r,
    ring_s, ring_r, all_s, all_r, twin_s, twin_r, row_s, row_r, back_s, back_r, sq_s, sq_r,
):
    bits_z = size_z.bit_length() - 1
    rows_gu, rows_down = 256 // size_z, 128 // size_z
    total_heads = 4 * size_x
    tok = lax.axis_index("tok")
    head_x = lax.axis_index("head")
    core = tok & 1
    z = (tok >> 1) & (size_z - 1)
    y = tok >> (1 + bits_z)
    own = (z - y) & 3

    def chip(dy, dz, dc=0):
        at_y = (y + dy) & (SIZE_Y - 1)
        at_z = (z + dz) & (size_z - 1)
        return {"tok": (at_y * size_z + at_z) * 2 + (core ^ dc)}

    def across(step):
        return {"head": (head_x + step) & (size_x - 1)}

    peers = sorted(range(1, size_z), key=lambda k: abs(k - size_z // 2))

    sources = {KEY: k_hbm, TGT: v_hbm, QRY: q_hbm}

    def load(kind, b):
        return pltpu.make_async_copy(sources[kind].at[b], raw.at[kind, b], load_sem.at[kind, b])

    barrier = pltpu.get_barrier_semaphore()
    greeted = [chip(k, k) for k in peers]
    greeted += [chip(dy, dz) for dy, dz, *_ in ROUTES]
    greeted += [across(s) for s in range(1, size_x)]
    greeted += [chip(0, 0, 1)]
    load(KEY, 0).start()
    load(TGT, 0).start()
    for device in greeted:
        pl.semaphore_signal(barrier, inc=1, device_id=device, device_id_type=MESH)
    w_load = pltpu.make_async_copy(w_hbm.at[own], weights, w_sem)
    small = [
        pltpu.make_async_copy(src, dst, small_sem.at[i])
        for i, (src, dst) in enumerate([(rate_hbm, rate_ref), (lr_hbm, lr_ref), (gain_hbm, gain_ref)])
    ]
    for copy in [small[0], w_load, small[1], small[2]]:
        copy.start()
    for kind, b in ((KEY, 1), (TGT, 1), (QRY, 0), (QRY, 1)):
        load(kind, b).start()

    rows_i = lax.broadcasted_iota(jnp.int32, (256, 256), 0)
    cols_i = lax.broadcasted_iota(jnp.int32, (256, 256), 1)

    def source_row(i):
        return (i & 31) * 8 + ((i >> 5) & 1) * 4 + (((i >> 6) + own) & 3)

    gather = jnp.where(source_row(rows_i) == cols_i, 1.0, 0.0).astype(BF)
    scatter = jnp.where(source_row(cols_i) == rows_i, 1.0, 0.0).astype(BF)

    def split_heads(kind, b):
        load(kind, b).wait()
        if kind == TGT:
            if b == 0:
                small[0].wait()
            rates = []
            for r in range(4):
                row = rate_ref[b, pl.ds((r + own) & 3, 1), :]
                rates.append(-jnp.transpose(jnp.broadcast_to(row, (128, 256))))
        for g in range(4):
            lo = raw[kind, b, 512 * g : 512 * g + 256, :]
            hi = raw[kind, b, 512 * g + 256 : 512 * g + 512, :]
            out = mm(gather, jnp.concatenate([lo, hi], axis=1))
            for r in range(4):
                for c in range(2):
                    for k in range(2):
                        t = 64 * g + 32 * k
                        tile = out[64 * r + 32 * c : 64 * r + 32 * c + 32, 128 * k : 128 * k + 128]
                        if kind == TGT:
                            tile = tile * rates[r][t : t + 32, :]
                        tile = tile.astype(BF)
                        cols = slice(128 * c, 128 * c + 128)
                        if kind == QRY and r == 0:
                            query[b, t : t + 32, cols] = tile
                        elif kind == QRY:
                            query_staged[b, r - 1, t : t + 32, cols] = tile
                        elif r == 0:
                            moved[b, 0, kind, t : t + 32, cols] = tile
                        else:
                            staged[b, kind, r - 1, t : t + 32, cols] = tile

    def remote(src, dst, s, r, device):
        return pltpu.make_async_remote_copy(
            src_ref=src, dst_ref=dst, send_sem=s, recv_sem=r, device_id=device, device_id_type=MESH
        )

    twin = chip(0, 0, 1)

    def moved_piece(b, i):
        dy, dz, r, t, row = ROUTES[i]
        return remote(
            staged.at[b, :, r - 1, pl.ds(t, HALF)],
            moved.at[b, 0, :, pl.ds(row, HALF)],
            move_s.at[b], move_r.at[b, i], chip(dy, dz),
        )

    def send_moved(b):
        for i in range(len(ROUTES)):
            moved_piece(b, i).start()

    def moved_all(b):
        return remote(staged.at[b], staged.at[b], move_s.at[b], move_r.at[b, 0], twin)

    def forward_rows(b, row, n):
        rows = pl.ds(row, n)
        return remote(moved.at[b, 0, :, rows], moved.at[b, 1, :, rows], fwd_s.at[b], fwd_r.at[b], twin)

    def send_own(b):
        forward_rows(b, 0, 256).start()

    def send_forward(b):
        for i in (2, 3, 4, 5, 0, 1):
            moved_piece(b, i).wait_recv()
            forward_rows(b, ROUTES[i][-1], HALF).start()

    def forward_all(b):
        return remote(moved.at[b, 0], moved.at[b, 1], fwd_s.at[b], fwd_r.at[b], twin)

    def send_query(b):
        for dy, dz, r, t, row in ROUTES:
            remote(
                query_staged.at[b, r - 1, pl.ds(t, HALF)], query.at[b, pl.ds(row, HALF)],
                query_s.at[b], query_r.at[b], chip(dy, dz),
            ).start()

    def query_all(b):
        return remote(query_staged.at[b], query_staged.at[b], query_s.at[b], query_r.at[b], twin)

    def gradients(b, s):
        for i in range(4):
            rows = slice(256 * i, 256 * i + 256)
            pre = mm(moved[b, s, KEY, rows, :], w_gu[...])
            gate_pre, up_pre = pre[:, :HALF], pre[:, HALF:]
            back = mm_nt(moved[b, s, TGT, rows, :], w_down[...])
            sg = jax.nn.sigmoid(gate_pre)
            act = gate_pre * sg
            hid[s, rows, :] = (act * up_pre).astype(BF)
            cots[s, rows, :HALF] = (back * up_pre * sg * (1.0 + gate_pre * (1.0 - sg))).astype(BF)
            cots[s, rows, HALF:] = (back * act).astype(BF)
        grad_gu = mm_tn(moved[b, s, KEY], cots[s]).reshape(size_z, rows_gu, 256)
        grad_down = mm_tn(hid[s], moved[b, s, TGT]).reshape(size_z, rows_down, 256)
        if s == 0:
            sums[:, :rows_gu, :] = grad_gu
            sums[:, rows_gu:, :] = grad_down
        else:
            grad_gu = sums[:, :rows_gu, :] + grad_gu
            grad_down = sums[:, rows_gu:, :] + grad_down
            sums[:, :rows_gu, :] = grad_gu
            sums[:, rows_gu:, :] = grad_down
            ring_src[b, :, :rows_gu, :] = grad_gu.astype(BF)
            ring_src[b, :, rows_gu:, :] = grad_down.astype(BF)

    def send_ring(b):
        for k in peers:
            remote(
                ring_src.at[b, (z + k) & (size_z - 1)], ring_dst.at[b, k - 1],
                ring_s.at[b], ring_r.at[b], chip(k, k),
            ).start()

    def ring_all(b):
        return remote(ring_dst.at[b], ring_dst.at[b], ring_s.at[b], ring_r.at[b], twin)

    def send_all(b):
        total = sums[z]
        for k in peers:
            total = total + ring_dst[b, k - 1].astype(F32)
        full[b, core, z] = total.astype(BF)
        for k in peers:
            remote(full.at[b, core, z], full.at[b, core, z], all_s.at[b], all_r.at[b], chip(k, k)).start()

    def all_all(b):
        return remote(ring_dst.at[b], ring_dst.at[b], all_s.at[b], all_r.at[b], twin)

    def twin_copy(b):
        return remote(full.at[b, core], full.at[b, core], twin_s.at[b], twin_r.at[b], twin)

    def send_twin(b):
        twin_copy(b).start()

    def set_weights(m, new):
        wide = new.astype(BF)
        weights_bf[m] = wide
        first = core == 0
        if m == 1:
            w_down[...] = jnp.where(first, new[:HALF, :], new[HALF:, :]).astype(BF)
        else:
            cols = slice(0, HALF) if m == 0 else slice(HALF, 256)
            w_gu[:, cols] = jnp.where(first, new[:, :HALF], new[:, HALF:]).astype(BF)

    def load_weights():
        w_load.wait()
        small[1].wait()
        small[2].wait()
        for m in range(3):
            set_weights(m, weights[m])

    def update(b):
        sides = [full[b, c, :, :rows_gu, :].reshape(256, 256) for c in range(2)]
        xs = [
            jnp.concatenate([side[:, :HALF] for side in sides], axis=1),
            jnp.concatenate([full[b, c, :, rows_gu:, :].reshape(HALF, 256) for c in range(2)], axis=0),
            jnp.concatenate([side[:, HALF:] for side in sides], axis=1),
        ]
        inverse = []
        for m in range(3):
            xf = xs[m].astype(F32)
            inverse.append(lax.rsqrt(jnp.sum(xf * xf, keepdims=True) + 1e-06))
        for step in range(NS_STEPS):
            grams = []
            for m in range(3):
                gram = mm_nt(xs[m], xs[m])
                if step == 0:
                    gram = gram * inverse[m] * inverse[m]
                grams.append(gram.astype(BF))
            polys = [
                (coef_b * grams[m].astype(F32) + coef_c * mm(grams[m], grams[m])).astype(BF) for m in range(3)
            ]
            for m in range(3):
                x = coef_a * xs[m].astype(F32) + mm(polys[m], xs[m])
                if step == 0:
                    x = x * inverse[m]
                xs[m] = x.astype(BF)
        for m in range(3):
            new = weights[m] - lr_ref[own, m] * xs[m].astype(F32)
            weights[m] = new
            set_weights(m, new)

    def apply(b, chunks):
        for i in chunks:
            rows = slice(256 * i, 256 * i + 256)
            gate = mm(query[b, rows, :], weights_bf[0])
            up = mm(query[b, rows, :], weights_bf[2])
            mapped = mm((gate * jax.nn.sigmoid(gate) * up).astype(BF), weights_bf[1])
            squares = mapped * mapped
            high = squares.astype(BF)
            low = (squares - high.astype(F32)).astype(BF)
            ones = jnp.ones((8, 256), BF)
            row_src[b, i] = mm_nt(ones, high) + mm_nt(ones, low)
            if i == 0:
                map_dst[b, 0] = mapped.astype(BF)
            else:
                map_src[b, i - 1] = mapped.astype(BF)

    def send_rows(b):
        for dy, dz, r, t, row in ROUTES:
            remote(
                row_src.at[b, row // 256, :, pl.ds(row % 256, HALF)], row_dst.at[b, r - 1, :, pl.ds(t, HALF)],
                row_s.at[b], row_r.at[b], chip(-dy, -dz),
            ).start()

    def rows_all(b):
        return remote(row_dst.at[b], row_dst.at[b], row_s.at[b], row_r.at[b], twin)

    def send_back(b):
        for dy, dz, r, t, row in ROUTES:
            remote(
                map_src.at[b, row // 256 - 1, pl.ds(row % 256, HALF)], map_dst.at[b, r, pl.ds(t, HALF)],
                back_s.at[b], back_r.at[b], chip(-dy, -dz),
            ).start()

    def back_all(b):
        return remote(map_src.at[b], map_src.at[b], back_s.at[b], back_r.at[b], twin)

    def send_squares(b):
        sq_src[b] = row_src[b, 0] + row_dst[b, 0] + row_dst[b, 1] + row_dst[b, 2]
        for s in range(1, size_x):
            remote(sq_src.at[b], sq_dst.at[b, s - 1], sq_s.at[b], sq_r.at[b], across(s)).start()

    def squares_all(b):
        return remote(sq_dst.at[b], sq_dst.at[b], sq_s.at[b], sq_r.at[b], twin)

    def store(b):
        return pltpu.make_async_copy(raw_out.at[b], out_hbm.at[b], store_sem.at[b])

    def finish(b):
        total = sq_src[b]
        for s in range(1, size_x):
            total = total + sq_dst[b, s - 1]
        scale = lax.rsqrt(total * (1.0 / (total_heads * 256)) + 1e-06)
        scale = jnp.transpose(jnp.broadcast_to(scale[0:1, :], (128, 256)))
        gains = [gain_ref[pl.ds((r + own) & 3, 1), :] for r in range(4)]
        for g in range(4):
            for r in range(4):
                for c in range(2):
                    for k in range(2):
                        t = 64 * g + 32 * k
                        cols = slice(128 * c, 128 * c + 128)
                        tile = map_dst[b, r, t : t + 32, cols].astype(F32) * scale[t : t + 32, :]
                        tile = tile * gains[r][:, cols]
                        tile_buf[g, 64 * r + 32 * c : 64 * r + 32 * c + 32, 128 * k : 128 * k + 128] = tile.astype(BF)
            out = mm(scatter, tile_buf[g]).astype(BF)
            raw_out[b, 512 * g : 512 * g + 256, :] = out[:, :128]
            raw_out[b, 512 * g + 256 : 512 * g + 512, :] = out[:, 128:]
        store(b).start()

    sent = []

    def send(start, whole, b):
        start(b)
        sent.append(whole(b))

    def got(copy):
        copy.wait_recv()

    def forward(b):
        send_forward(b)
        sent.append(forward_all(b))

    def later_queries():
        send(send_query, query_all, 0)
        send(send_query, query_all, 1)

    def serve(b):
        apply(b, (3, 1, 2))
        send(send_rows, rows_all, b)
        send(send_back, back_all, b)
        apply(b, (0,))

    steps = [
        lambda: split_heads(KEY, 0),
        lambda: split_heads(TGT, 0),
        lambda: pl.semaphore_wait(barrier, len(greeted)),
        lambda: send(send_moved, moved_all, 0),
        lambda: send_own(0),
        load_weights,
        lambda: split_heads(KEY, 1),
        lambda: split_heads(TGT, 1),
        lambda: split_heads(QRY, 0),
        lambda: split_heads(QRY, 1),
        lambda: send_own(1),
        lambda: forward(0),
        lambda: gradients(0, 0),
        lambda: got(forward_all(0)),
        lambda: gradients(0, 1),
        lambda: send(send_ring, ring_all, 0),
        lambda: send(send_moved, moved_all, 1),
        lambda: got(ring_all(0)),
        lambda: send(send_all, all_all, 0),
        later_queries,
        lambda: forward(1),
        lambda: got(all_all(0)),
        lambda: send(send_twin, twin_copy, 0),
        lambda: got(twin_copy(0)),
        lambda: update(0),
        lambda: got(forward_all(1)),
        lambda: gradients(1, 0),
        lambda: gradients(1, 1),
        lambda: send(send_ring, ring_all, 1),
        lambda: got(query_all(0)),
        lambda: serve(0),
        lambda: got(ring_all(1)),
        lambda: send(send_all, all_all, 1),
        lambda: got(rows_all(0)),
        lambda: send(send_squares, squares_all, 0),
        lambda: got(squares_all(0)),
        lambda: got(back_all(0)),
        lambda: finish(0),
        lambda: got(all_all(1)),
        lambda: send(send_twin, twin_copy, 1),
        lambda: got(twin_copy(1)),
        lambda: update(1),
        lambda: got(query_all(1)),
        lambda: serve(1),
        lambda: got(rows_all(1)),
        lambda: send(send_squares, squares_all, 1),
        lambda: got(back_all(1)),
        lambda: got(squares_all(1)),
        lambda: finish(1),
        lambda: store(0).wait(),
        lambda: store(1).wait(),
    ]
    for step in steps:
        step()
    for copy in sent:
        copy.wait_send()


def per_device(size_z, size_x, queries, key_input, value_input, token_rates, fast_weights, update_rate, out_gain):
    piece = 384 // size_z

    def flat(a):
        return a.reshape(2, 256, 4, 2, 128).transpose(0, 1, 3, 2, 4).reshape(2, 2048, 128)

    hbm = pl.BlockSpec(memory_space=pltpu.HBM)
    dma = pltpu.SemaphoreType.DMA
    out = pl.pallas_call(
        functools.partial(kernel, size_z, size_x),
        out_shape=jax.ShapeDtypeStruct((2, 2048, 128), BF),
        in_specs=[hbm] * 7,
        out_specs=hbm,
        scratch_shapes=[
            pltpu.VMEM((3, 2, 2048, 128), BF),
            pltpu.VMEM((2, 4, 256), F32),
            pltpu.SMEM((4, 3), F32),
            pltpu.VMEM((4, 256), F32),
            pltpu.VMEM((2, 2048, 128), BF),
            pltpu.VMEM((2, 2, 2, 1024, 256), BF),
            pltpu.VMEM((2, 2, 3, 256, 256), BF),
            pltpu.VMEM((2, 1024, 256), BF),
            pltpu.VMEM((2, 3, 256, 256), BF),
            pltpu.VMEM((3, 256, 256), F32),
            pltpu.VMEM((3, 256, 256), BF),
            pltpu.VMEM((256, 256), BF),
            pltpu.VMEM((128, 256), BF),
            pltpu.VMEM((2, 1024, 128), BF),
            pltpu.VMEM((2, 1024, 256), BF),
            pltpu.VMEM((size_z, piece, 256), F32),
            pltpu.VMEM((2, size_z, piece, 256), BF),
            pltpu.VMEM((2, size_z - 1, piece, 256), BF),
            pltpu.VMEM((2, 2, size_z, piece, 256), BF),
            pltpu.VMEM((2, 3, 256, 256), BF),
            pltpu.VMEM((2, 4, 256, 256), BF),
            pltpu.VMEM((4, 256, 256), BF),
            pltpu.VMEM((2, 4, 8, 256), F32),
            pltpu.VMEM((2, 3, 8, 256), F32),
            pltpu.VMEM((2, 8, 256), F32),
            pltpu.VMEM((2, max(size_x - 1, 1), 8, 256), F32),
            dma((3, 2)), dma, dma((3,)), dma((2,)),
            dma((2,)), dma((2, len(ROUTES))),
            *[dma((2,)) for _ in range(16)],
        ],
        compiler_params=pltpu.CompilerParams(
            collective_id=0, has_side_effects=True, vmem_limit_bytes=60 * 1024 * 1024
        ),
        cost_estimate=pl.CostEstimate(flops=12_000_000_000, bytes_accessed=5_000_000, transcendentals=1_000_000),
    )(flat(queries), flat(key_input), flat(value_input), token_rates, fast_weights, update_rate, out_gain)
    return out.reshape(2, 256, 2, 4, 128).transpose(0, 1, 3, 2, 4).reshape(2, 256, 4, 256)


def solution(mesh):
    size_z = mesh.shape["tok"] // (2 * SIZE_Y)
    return jax.shard_map(
        functools.partial(per_device, size_z, mesh.shape["head"]),
        mesh=mesh,
        in_specs=(
            P(None, "tok", "head", None),
            P(None, "tok", "head", None),
            P(None, "tok", "head", None),
            P(None, "head", "tok"),
            P("head", None, None, None),
            P("head", None),
            P("head", None),
        ),
        out_specs=P(None, "tok", "head", None),
        check_vma=False,
    )
```

```python
import functools

import jax
import jax.numpy as jnp
from jax import lax
from jax.experimental import pallas as pl
from jax.experimental.pallas import tpu as pltpu
from jax.sharding import PartitionSpec as P

NS_STEPS = 3
SIZE_Y = 4

coef_a = 3.4445
coef_b = -4.775
coef_c = 2.0315

BF = jnp.bfloat16
F32 = jnp.float32
MESH = pl.DeviceIdType.MESH
KEY, TGT, QRY = 0, 1, 2
HALF = 128

ROUTES = (
    (-1, 1, 2, 0, 768),
    (1, -1, 2, 128, 896),
    (0, 1, 1, 0, 256),
    (-1, 0, 1, 128, 384),
    (0, -1, 3, 0, 512),
    (1, 0, 3, 128, 640),
)
MOVES = (
    (-1, 1, 2, 0, 128, 768),
    (1, -1, 2, 128, 128, 896),
    (0, 1, 1, 0, 128, 256),
    (-1, 0, 1, 128, 128, 384),
    (0, -1, 3, 0, 128, 512),
    (1, 0, 3, 128, 128, 640),
)


def mm(a, b):
    return jnp.dot(a, b, preferred_element_type=F32)


def mm_nt(a, b):
    return lax.dot_general(a, b, (((1,), (1,)), ((), ())), preferred_element_type=F32)


def mm_tn(a, b):
    return lax.dot_general(a, b, (((0,), (0,)), ((), ())), preferred_element_type=F32)


def kernel(
    size_z, size_x,
    q_hbm, k_hbm, v_hbm, w_hbm, small_ref, out_ref,
    raw, laid, moved, staged, query, query_staged,
    weights, weights_bf, w_gu, w_down, hid, cots, sums, ring_src, ring_dst, full,
    map_src, map_dst, tile_buf, row_src, row_dst, sq_src, sq_dst,
    near_sem, far_sem, load_sem, w_sem, move_s, move_r, fwd_s, fwd_r, query_s, query_r,
    ring_s, ring_r, all_s, all_r, twin_s, twin_r, row_s, row_r, back_s, back_r, sq_s, sq_r,
):
    bits_z = size_z.bit_length() - 1
    rows_gu, rows_down = 256 // size_z, 128 // size_z
    total_heads = 4 * size_x
    tok = lax.axis_index("tok")
    head_x = lax.axis_index("head")
    core = tok & 1
    z = (tok >> 1) & (size_z - 1)
    y = tok >> (1 + bits_z)
    own = (z - y) & 3

    def chip(dy, dz, dc=0):
        at_y = (y + dy) & (SIZE_Y - 1)
        at_z = (z + dz) & (size_z - 1)
        return {"tok": (at_y * size_z + at_z) * 2 + (core ^ dc)}

    def across(step):
        return {"head": (head_x + step) & (size_x - 1)}

    peers = sorted(range(1, size_z), key=lambda k: abs(k - size_z // 2))

    sources = {KEY: k_hbm, TGT: v_hbm, QRY: q_hbm}

    def load(kind, b):
        return pltpu.make_async_copy(sources[kind].at[b], raw.at[kind, b], load_sem.at[kind, b])

    barrier = pltpu.get_barrier_semaphore()
    near = [chip(dy, dz) for dy, dz, *_ in ROUTES]
    greeted = [*near]
    greeted += [across(s) for s in range(1, size_x)]
    greeted += [chip(0, 0, 1)]
    load(KEY, 0).start()
    load(TGT, 0).start()
    for device in greeted:
        pl.semaphore_signal(barrier, inc=1, device_id=device, device_id_type=MESH)
    w_load = pltpu.make_async_copy(w_hbm.at[own], weights, w_sem)
    w_load.start()
    for kind, b in ((KEY, 1), (TGT, 1), (QRY, 0), (QRY, 1)):
        load(kind, b).start()

    def signal_near():
        for device in near:
            pl.semaphore_signal(near_sem, inc=1, device_id=device, device_id_type=MESH)

    def signal_far():
        pl.semaphore_wait(near_sem, len(near))
        for dz in (2, -2):
            pl.semaphore_signal(far_sem, inc=1, device_id=chip(0, dz), device_id_type=MESH)

    rows_i = lax.broadcasted_iota(jnp.int32, (256, 256), 0)
    cols_i = lax.broadcasted_iota(jnp.int32, (256, 256), 1)

    def source_row(i):
        return (i & 31) * 8 + ((i >> 5) & 1) * 4 + (((i >> 6) + own) & 3)

    gather = jnp.where(source_row(rows_i) == cols_i, 1.0, 0.0).astype(BF)
    scatter = jnp.where(source_row(cols_i) == rows_i, 1.0, 0.0).astype(BF)

    def split_heads(kind, b):
        load(kind, b).wait()
        if kind == TGT:
            rates = []
            for r in range(4):
                row = small_ref[b, pl.ds((r + own) & 3, 1), :]
                rates.append(-jnp.transpose(jnp.broadcast_to(row, (128, 256))))
        for g in range(4):
            lo = raw[kind, b, 512 * g : 512 * g + 256, :]
            hi = raw[kind, b, 512 * g + 256 : 512 * g + 512, :]
            out = mm(gather, jnp.concatenate([lo, hi], axis=1))
            for r in range(4):
                for c in range(2):
                    for k in range(2):
                        t = 64 * g + 32 * k
                        tile = out[64 * r + 32 * c : 64 * r + 32 * c + 32, 128 * k : 128 * k + 128]
                        if kind == TGT:
                            tile = tile * rates[r][t : t + 32, :]
                        tile = tile.astype(BF)
                        cols = slice(128 * c, 128 * c + 128)
                        if kind == QRY and r == 0:
                            query[b, t : t + 32, cols] = tile
                        elif kind == QRY:
                            query_staged[b, r - 1, t : t + 32, cols] = tile
                        elif r == 0:
                            moved[b, 0, kind, t : t + 32, cols] = tile
                        else:
                            staged[b, kind, r - 1, t : t + 32, cols] = tile

    def remote(src, dst, s, r, device):
        return pltpu.make_async_remote_copy(
            src_ref=src, dst_ref=dst, send_sem=s, recv_sem=r, device_id=device, device_id_type=MESH
        )

    twin = chip(0, 0, 1)

    def moved_piece(b, i):
        dy, dz, r, t, n, row = MOVES[i]
        return remote(
            staged.at[b, :, r - 1, pl.ds(t, n)],
            moved.at[b, 0, :, pl.ds(row, n)],
            move_s.at[b], move_r.at[b, i], chip(dy, dz),
        )

    def send_moved(b):
        for i in range(len(MOVES)):
            moved_piece(b, i).start()

    def moved_all(b):
        return remote(staged.at[b], staged.at[b], move_s.at[b], move_r.at[b, 0], twin)

    def forward_rows(b, at, row, n):
        rows = pl.ds(row, n)
        return remote(moved.at[b, 0, :, rows], moved.at[b, 1, :, rows], fwd_s.at[b], fwd_r.at[b, at], twin)

    def send_own(b):
        forward_rows(b, 0, 0, 256).start()

    def pass_on(b, at):
        for i, (*_, n, row) in enumerate(MOVES):
            if row // 256 == at:
                moved_piece(b, i).wait_recv()
                forward_rows(b, at, row, n).start()

    def passed(b, at):
        forward_rows(b, at, 256 * at, 256).wait_recv()

    def forward_all(b):
        return remote(moved.at[b, 0], moved.at[b, 1], fwd_s.at[b], fwd_r.at[b, 0], twin)

    def send_query(b):
        for dy, dz, r, t, row in ROUTES:
            remote(
                query_staged.at[b, r - 1, pl.ds(t, HALF)], query.at[b, pl.ds(row, HALF)],
                query_s.at[b], query_r.at[b], chip(dy, dz),
            ).start()

    def query_all(b):
        return remote(query_staged.at[b], query_staged.at[b], query_s.at[b], query_r.at[b], twin)

    def gradients(b, s, chunks=range(4), opens=False, closes=False):
        all_rows = slice(256 * chunks[0], 256 * chunks[-1] + 256)
        for i in chunks:
            rows = slice(256 * i, 256 * i + 256)
            pre = mm(moved[b, s, KEY, rows, :], w_gu[...])
            gate_pre, up_pre = pre[:, :HALF], pre[:, HALF:]
            back = mm_nt(moved[b, s, TGT, rows, :], w_down[...])
            sg = jax.nn.sigmoid(gate_pre)
            act = gate_pre * sg
            hid[s, rows, :] = (act * up_pre).astype(BF)
            cots[s, rows, :HALF] = (back * up_pre * sg * (1.0 + gate_pre * (1.0 - sg))).astype(BF)
            cots[s, rows, HALF:] = (back * act).astype(BF)
        grad_gu = mm_tn(moved[b, s, KEY, all_rows, :], cots[s, all_rows, :]).reshape(size_z, rows_gu, 256)
        grad_down = mm_tn(hid[s, all_rows, :], moved[b, s, TGT, all_rows, :]).reshape(size_z, rows_down, 256)
        if not opens:
            grad_gu = sums[:, :rows_gu, :] + grad_gu
            grad_down = sums[:, rows_gu:, :] + grad_down
        sums[:, :rows_gu, :] = grad_gu
        sums[:, rows_gu:, :] = grad_down
        if closes:
            ring_src[b, :, :rows_gu, :] = grad_gu.astype(BF)
            ring_src[b, :, rows_gu:, :] = grad_down.astype(BF)

    def send_ring(b):
        for k in peers:
            remote(
                ring_src.at[b, (z + k) & (size_z - 1)], ring_dst.at[b, k - 1],
                ring_s.at[b], ring_r.at[b], chip(k, k),
            ).start()

    def ring_all(b):
        return remote(ring_dst.at[b], ring_dst.at[b], ring_s.at[b], ring_r.at[b], twin)

    def send_all(b):
        total = sums[z]
        for k in peers:
            total = total + ring_dst[b, k - 1].astype(F32)
        full[b, core, z] = total.astype(BF)
        for k in peers:
            remote(full.at[b, core, z], full.at[b, core, z], all_s.at[b], all_r.at[b], chip(k, k)).start()

    def all_all(b):
        return remote(ring_dst.at[b], ring_dst.at[b], all_s.at[b], all_r.at[b], twin)

    def twin_copy(b):
        return remote(full.at[b, core], full.at[b, core], twin_s.at[b], twin_r.at[b], twin)

    def send_twin(b):
        twin_copy(b).start()

    def set_weights(m, new):
        wide = new.astype(BF)
        weights_bf[m] = wide
        first = core == 0
        if m == 1:
            w_down[...] = jnp.where(first, new[:HALF, :], new[HALF:, :]).astype(BF)
        else:
            cols = slice(0, HALF) if m == 0 else slice(HALF, 256)
            w_gu[:, cols] = jnp.where(first, new[:, :HALF], new[:, HALF:]).astype(BF)

    def load_weights():
        w_load.wait()
        for m in range(3):
            set_weights(m, weights[m])

    def update(b):
        sides = [full[b, c, :, :rows_gu, :].reshape(256, 256) for c in range(2)]
        xs = [
            jnp.concatenate([side[:, :HALF] for side in sides], axis=1),
            jnp.concatenate([full[b, c, :, rows_gu:, :].reshape(HALF, 256) for c in range(2)], axis=0),
            jnp.concatenate([side[:, HALF:] for side in sides], axis=1),
        ]
        inverse = []
        for m in range(3):
            xf = xs[m].astype(F32)
            inverse.append(lax.rsqrt(jnp.sum(xf * xf, keepdims=True) + 1e-06))
        for step in range(NS_STEPS):
            grams = []
            for m in range(3):
                gram = mm_nt(xs[m], xs[m])
                if step == 0:
                    gram = gram * inverse[m] * inverse[m]
                grams.append(gram.astype(BF))
            polys = [
                (coef_b * grams[m].astype(F32) + coef_c * mm(grams[m], grams[m])).astype(BF) for m in range(3)
            ]
            for m in range(3):
                x = coef_a * xs[m].astype(F32) + mm(polys[m], xs[m])
                if step == 0:
                    x = x * inverse[m]
                xs[m] = x.astype(BF)
        for m in range(3):
            new = weights[m] - small_ref[3, pl.ds(own, 1), :][:, m : m + 1] * xs[m].astype(F32)
            weights[m] = new
            set_weights(m, new)

    def apply(b, chunks):
        for i in chunks:
            rows = slice(256 * i, 256 * i + 256)
            gate = mm(query[b, rows, :], weights_bf[0])
            up = mm(query[b, rows, :], weights_bf[2])
            mapped = mm((gate * jax.nn.sigmoid(gate) * up).astype(BF), weights_bf[1])
            squares = mapped * mapped
            high = squares.astype(BF)
            low = (squares - high.astype(F32)).astype(BF)
            ones = jnp.ones((8, 256), BF)
            row_src[b, i] = mm_nt(ones, high) + mm_nt(ones, low)
            if i == 0:
                map_dst[b, 0] = mapped.astype(BF)
            else:
                map_src[b, i - 1] = mapped.astype(BF)

    def send_rows(b):
        for dy, dz, r, t, row in ROUTES:
            remote(
                row_src.at[b, row // 256, :, pl.ds(row % 256, HALF)], row_dst.at[b, r - 1, :, pl.ds(t, HALF)],
                row_s.at[b], row_r.at[b], chip(-dy, -dz),
            ).start()

    def rows_all(b):
        return remote(row_dst.at[b], row_dst.at[b], row_s.at[b], row_r.at[b], twin)

    def send_back(b):
        for dy, dz, r, t, row in ROUTES:
            remote(
                map_src.at[b, row // 256 - 1, pl.ds(row % 256, HALF)], map_dst.at[b, r, pl.ds(t, HALF)],
                back_s.at[b], back_r.at[b], chip(-dy, -dz),
            ).start()

    def back_all(b):
        return remote(map_src.at[b], map_src.at[b], back_s.at[b], back_r.at[b], twin)

    def send_squares(b):
        sq_src[b] = row_src[b, 0] + row_dst[b, 0] + row_dst[b, 1] + row_dst[b, 2]
        for s in range(1, size_x):
            remote(sq_src.at[b], sq_dst.at[b, s - 1], sq_s.at[b], sq_r.at[b], across(s)).start()

    def squares_all(b):
        return remote(sq_dst.at[b], sq_dst.at[b], sq_s.at[b], sq_r.at[b], twin)

    def lay_out(b):
        for g in range(4):
            for r in range(4):
                for c in range(2):
                    for k in range(2):
                        t = 64 * g + 32 * k
                        tile_buf[g, 64 * r + 32 * c : 64 * r + 32 * c + 32, 128 * k : 128 * k + 128] = map_dst[
                            b, r, t : t + 32, 128 * c : 128 * c + 128
                        ]
            out = mm(scatter, tile_buf[g]).astype(BF)
            laid[b, 512 * g : 512 * g + 256, :] = out[:, :128]
            laid[b, 512 * g + 256 : 512 * g + 512, :] = out[:, 128:]

    def finish(b):
        total = sq_src[b]
        for s in range(1, size_x):
            total = total + sq_dst[b, s - 1]
        scale = lax.rsqrt(total * (1.0 / (total_heads * 256)) + 1e-06)
        scale = jnp.transpose(jnp.broadcast_to(scale[0:1, :], (128, 256)))
        gain = jnp.concatenate([small_ref[2, :, :128], small_ref[2, :, 128:]], axis=0)
        out = laid[b].astype(F32).reshape(256, 8, 128) * scale[:, None, :] * gain[None, :, :]
        out_ref[b] = out.reshape(2048, 128).astype(BF)

    sent = []

    def send(start, whole, b):
        start(b)
        sent.append(whole(b))

    def got(copy):
        copy.wait_recv()

    def first_gradients():
        sent.append(forward_all(0))
        for at in (1, 2, 3):
            pass_on(0, at)
        gradients(0, 0, opens=True)
        for at in range(4):
            passed(0, at)
        gradients(0, 1, closes=True)

    def later_tokens():
        for at in (1, 2, 3):
            pass_on(1, at)
        sent.append(forward_all(1))

    def later_queries():
        send(send_query, query_all, 0)
        send(send_query, query_all, 1)

    def serve(b):
        apply(b, (3, 1, 2))
        send(send_rows, rows_all, b)
        send(send_back, back_all, b)
        apply(b, (0,))

    steps = [
        lambda: split_heads(KEY, 0),
        lambda: split_heads(TGT, 0),
        lambda: pl.semaphore_wait(barrier, len(greeted)),
        lambda: send(send_moved, moved_all, 0),
        lambda: send_own(0),
        signal_near,
        load_weights,
        lambda: split_heads(KEY, 1),
        lambda: split_heads(TGT, 1),
        signal_far,
        lambda: split_heads(QRY, 0),
        lambda: split_heads(QRY, 1),
        lambda: send_own(1),
        first_gradients,
        lambda: pl.semaphore_wait(far_sem, 2),
        lambda: send(send_ring, ring_all, 0),
        lambda: send(send_moved, moved_all, 1),
        lambda: got(ring_all(0)),
        lambda: send(send_all, all_all, 0),
        later_queries,
        later_tokens,
        lambda: got(all_all(0)),
        lambda: send(send_twin, twin_copy, 0),
        lambda: got(twin_copy(0)),
        lambda: update(0),
        lambda: [passed(1, at) for at in range(4)],
        lambda: gradients(1, 0, opens=True),
        lambda: gradients(1, 1, closes=True),
        lambda: send(send_ring, ring_all, 1),
        lambda: got(query_all(0)),
        lambda: serve(0),
        lambda: got(ring_all(1)),
        lambda: send(send_all, all_all, 1),
        lambda: got(rows_all(0)),
        lambda: send(send_squares, squares_all, 0),
        lambda: got(back_all(0)),
        lambda: lay_out(0),
        lambda: got(squares_all(0)),
        lambda: finish(0),
        lambda: got(all_all(1)),
        lambda: send(send_twin, twin_copy, 1),
        lambda: got(twin_copy(1)),
        lambda: update(1),
        lambda: got(query_all(1)),
        lambda: serve(1),
        lambda: got(rows_all(1)),
        lambda: send(send_squares, squares_all, 1),
        lambda: got(back_all(1)),
        lambda: lay_out(1),
        lambda: got(squares_all(1)),
        lambda: finish(1),
    ]
    for step in steps:
        step()
    for copy in sent:
        copy.wait_send()


def per_device(size_z, size_x, queries, key_input, value_input, token_rates, fast_weights, update_rate, out_gain):
    piece = 384 // size_z

    def flat(a):
        return a.reshape(2, 256, 4, 2, 128).transpose(0, 1, 3, 2, 4).reshape(2, 2048, 128)

    small = jnp.concatenate(
        [token_rates, out_gain[None], jnp.pad(update_rate, ((0, 0), (0, 253)))[None]], axis=0
    )
    hbm = pl.BlockSpec(memory_space=pltpu.HBM)
    dma = pltpu.SemaphoreType.DMA
    out = pl.pallas_call(
        functools.partial(kernel, size_z, size_x),
        out_shape=jax.ShapeDtypeStruct((2, 2048, 128), BF),
        in_specs=[hbm] * 4 + [pl.BlockSpec(memory_space=pltpu.VMEM)],
        out_specs=pl.BlockSpec(memory_space=pltpu.VMEM),
        scratch_shapes=[
            pltpu.VMEM((3, 2, 2048, 128), BF),
            pltpu.VMEM((2, 2048, 128), BF),
            pltpu.VMEM((2, 2, 2, 1024, 256), BF),
            pltpu.VMEM((2, 2, 3, 256, 256), BF),
            pltpu.VMEM((2, 1024, 256), BF),
            pltpu.VMEM((2, 3, 256, 256), BF),
            pltpu.VMEM((3, 256, 256), F32),
            pltpu.VMEM((3, 256, 256), BF),
            pltpu.VMEM((256, 256), BF),
            pltpu.VMEM((128, 256), BF),
            pltpu.VMEM((2, 1024, 128), BF),
            pltpu.VMEM((2, 1024, 256), BF),
            pltpu.VMEM((size_z, piece, 256), F32),
            pltpu.VMEM((2, size_z, piece, 256), BF),
            pltpu.VMEM((2, size_z - 1, piece, 256), BF),
            pltpu.VMEM((2, 2, size_z, piece, 256), BF),
            pltpu.VMEM((2, 3, 256, 256), BF),
            pltpu.VMEM((2, 4, 256, 256), BF),
            pltpu.VMEM((4, 256, 256), BF),
            pltpu.VMEM((2, 4, 8, 256), F32),
            pltpu.VMEM((2, 3, 8, 256), F32),
            pltpu.VMEM((2, 8, 256), F32),
            pltpu.VMEM((2, max(size_x - 1, 1), 8, 256), F32),
            pltpu.SemaphoreType.REGULAR, pltpu.SemaphoreType.REGULAR,
            dma((3, 2)), dma,
            dma((2,)), dma((2, len(MOVES))), dma((2,)), dma((2, 4)),
            *[dma((2,)) for _ in range(14)],
        ],
        compiler_params=pltpu.CompilerParams(
            collective_id=0, has_side_effects=True, vmem_limit_bytes=53760 * 1024
        ),
        cost_estimate=pl.CostEstimate(flops=12_000_000_000, bytes_accessed=5_000_000, transcendentals=1_000_000),
    )(flat(queries), flat(key_input), flat(value_input), fast_weights, small)
    return out.reshape(2, 256, 2, 4, 128).transpose(0, 1, 3, 2, 4).reshape(2, 256, 4, 256)


def solution(mesh):
    size_z = mesh.shape["tok"] // (2 * SIZE_Y)
    return jax.shard_map(
        functools.partial(per_device, size_z, mesh.shape["head"]),
        mesh=mesh,
        in_specs=(
            P(None, "tok", "head", None),
            P(None, "tok", "head", None),
            P(None, "tok", "head", None),
            P(None, "head", "tok"),
            P("head", None, None, None),
            P("head", None),
            P("head", None),
        ),
        out_specs=P(None, "tok", "head", None),
        check_vma=False,
    )
```

```python
import functools

import jax
import jax.numpy as jnp
from jax import lax
from jax.experimental import pallas as pl
from jax.experimental.pallas import tpu as pltpu
from jax.sharding import PartitionSpec as P

NS_STEPS = 3
SIZE_Y = 4

coef_a = 3.4445
coef_b = -4.775
coef_c = 2.0315

BF = jnp.bfloat16
F32 = jnp.float32
MESH = pl.DeviceIdType.MESH
KEY, TGT, QRY = 0, 1, 2
HALF = 128

ROUTES = (
    (-1, 1, 2, 0, 768),
    (1, -1, 2, 128, 896),
    (0, 1, 1, 0, 256),
    (-1, 0, 1, 128, 384),
    (0, -1, 3, 0, 512),
    (1, 0, 3, 128, 640),
)
MOVES = (
    (-1, 1, 2, 0, 128, 768),
    (1, -1, 2, 128, 128, 896),
    (0, 1, 1, 0, 128, 256),
    (-1, 0, 1, 128, 128, 384),
    (0, -1, 3, 0, 128, 512),
    (1, 0, 3, 128, 128, 640),
)


def mm(a, b):
    return jnp.dot(a, b, preferred_element_type=F32)


def mm_nt(a, b):
    return lax.dot_general(a, b, (((1,), (1,)), ((), ())), preferred_element_type=F32)


def mm_tn(a, b):
    return lax.dot_general(a, b, (((0,), (0,)), ((), ())), preferred_element_type=F32)


def kernel(
    size_z, size_x,
    q_hbm, k_hbm, v_hbm, w_hbm, small_ref, out_ref,
    raw, laid, moved, staged, query, query_staged,
    weights, weights_bf, w_gu, w_down, hid, cots, sums, ring_src, ring_dst, full,
    map_src, map_dst, tile_buf, row_src, row_dst, sq_src, sq_dst,
    near_sem, far_sem, load_sem, w_sem, move_s, move_r, fwd_s, fwd_r, query_s, query_r,
    ring_s, ring_r, all_s, all_r, twin_s, twin_r, row_s, row_r, back_s, back_r, sq_s, sq_r,
):
    bits_z = size_z.bit_length() - 1
    rows_gu, rows_down = 256 // size_z, 128 // size_z
    total_heads = 4 * size_x
    tok = lax.axis_index("tok")
    head_x = lax.axis_index("head")
    core = tok & 1
    z = (tok >> 1) & (size_z - 1)
    y = tok >> (1 + bits_z)
    own = (z - y) & 3

    def chip(dy, dz, dc=0):
        at_y = (y + dy) & (SIZE_Y - 1)
        at_z = (z + dz) & (size_z - 1)
        return {"tok": (at_y * size_z + at_z) * 2 + (core ^ dc)}

    def across(step):
        return {"head": (head_x + step) & (size_x - 1)}

    peers = sorted(range(1, size_z), key=lambda k: abs(k - size_z // 2))

    sources = {KEY: k_hbm, TGT: v_hbm, QRY: q_hbm}

    def load(kind, b):
        return pltpu.make_async_copy(sources[kind].at[b], raw.at[kind, b], load_sem.at[kind, b])

    barrier = pltpu.get_barrier_semaphore()
    near = [chip(dy, dz) for dy, dz, *_ in ROUTES]
    greeted = [*near]
    greeted += [across(s) for s in range(1, size_x)]
    greeted += [chip(0, 0, 1)]
    load(KEY, 0).start()
    load(TGT, 0).start()
    for device in greeted:
        pl.semaphore_signal(barrier, inc=1, device_id=device, device_id_type=MESH)
    w_load = pltpu.make_async_copy(w_hbm.at[own], weights, w_sem)
    w_load.start()
    for kind, b in ((KEY, 1), (TGT, 1), (QRY, 0), (QRY, 1)):
        load(kind, b).start()

    def signal_near():
        for device in near:
            pl.semaphore_signal(near_sem, inc=1, device_id=device, device_id_type=MESH)

    def signal_far():
        pl.semaphore_wait(near_sem, len(near))
        for dz in (2, -2):
            pl.semaphore_signal(far_sem, inc=1, device_id=chip(0, dz), device_id_type=MESH)

    rows_i = lax.broadcasted_iota(jnp.int32, (256, 256), 0)
    cols_i = lax.broadcasted_iota(jnp.int32, (256, 256), 1)

    def source_row(i):
        return (i & 31) * 8 + ((i >> 5) & 1) * 4 + (((i >> 6) + own) & 3)

    gather = jnp.where(source_row(rows_i) == cols_i, 1.0, 0.0).astype(BF)
    scatter = jnp.where(source_row(cols_i) == rows_i, 1.0, 0.0).astype(BF)

    def split_heads(kind, b):
        load(kind, b).wait()
        if kind == TGT:
            rates = []
            for r in range(4):
                row = small_ref[b, pl.ds((r + own) & 3, 1), :]
                rates.append(-jnp.transpose(jnp.broadcast_to(row, (128, 256))))
        for g in range(4):
            lo = raw[kind, b, 512 * g : 512 * g + 256, :]
            hi = raw[kind, b, 512 * g + 256 : 512 * g + 512, :]
            out = mm(gather, jnp.concatenate([lo, hi], axis=1))
            for r in range(4):
                for c in range(2):
                    for k in range(2):
                        t = 64 * g + 32 * k
                        tile = out[64 * r + 32 * c : 64 * r + 32 * c + 32, 128 * k : 128 * k + 128]
                        if kind == TGT:
                            tile = tile * rates[r][t : t + 32, :]
                        tile = tile.astype(BF)
                        cols = slice(128 * c, 128 * c + 128)
                        if kind == QRY and r == 0:
                            query[b, t : t + 32, cols] = tile
                        elif kind == QRY:
                            query_staged[b, r - 1, t : t + 32, cols] = tile
                        elif r == 0:
                            moved[b, 0, kind, t : t + 32, cols] = tile
                        else:
                            staged[b, kind, r - 1, t : t + 32, cols] = tile

    def remote(src, dst, s, r, device):
        return pltpu.make_async_remote_copy(
            src_ref=src, dst_ref=dst, send_sem=s, recv_sem=r, device_id=device, device_id_type=MESH
        )

    twin = chip(0, 0, 1)

    def moved_piece(b, i):
        dy, dz, r, t, n, row = MOVES[i]
        return remote(
            staged.at[b, :, r - 1, pl.ds(t, n)],
            moved.at[b, 0, :, pl.ds(row, n)],
            move_s.at[b], move_r.at[b, i], chip(dy, dz),
        )

    def send_kind(kind, b):
        for i, (dy, dz, r, t, n, row) in enumerate(MOVES):
            remote(
                staged.at[b, kind, r - 1, pl.ds(t, n)],
                moved.at[b, 0, kind, pl.ds(row, n)],
                move_s.at[b], move_r.at[b, i], chip(dy, dz),
            ).start()

    def send_moved(b):
        send_kind(KEY, b)
        send_kind(TGT, b)

    def moved_all(b):
        return remote(staged.at[b], staged.at[b], move_s.at[b], move_r.at[b, 0], twin)

    def forward_rows(b, at, row, n):
        rows = pl.ds(row, n)
        return remote(moved.at[b, 0, :, rows], moved.at[b, 1, :, rows], fwd_s.at[b], fwd_r.at[b, at], twin)

    def send_own(b):
        forward_rows(b, 0, 0, 256).start()

    def pass_on(b, at):
        for i, (*_, n, row) in enumerate(MOVES):
            if row // 256 == at:
                moved_piece(b, i).wait_recv()
                forward_rows(b, at, row, n).start()

    def passed(b, at):
        forward_rows(b, at, 256 * at, 256).wait_recv()

    def forward_all(b):
        return remote(moved.at[b, 0], moved.at[b, 1], fwd_s.at[b], fwd_r.at[b, 0], twin)

    def send_query(b):
        for dy, dz, r, t, row in ROUTES:
            remote(
                query_staged.at[b, r - 1, pl.ds(t, HALF)], query.at[b, pl.ds(row, HALF)],
                query_s.at[b], query_r.at[b], chip(dy, dz),
            ).start()

    def query_all(b):
        return remote(query_staged.at[b], query_staged.at[b], query_s.at[b], query_r.at[b], twin)

    def gradients(b, s, chunks=range(4), opens=False, closes=False):
        all_rows = slice(256 * chunks[0], 256 * chunks[-1] + 256)
        for i in chunks:
            rows = slice(256 * i, 256 * i + 256)
            pre = mm(moved[b, s, KEY, rows, :], w_gu[...])
            gate_pre, up_pre = pre[:, :HALF], pre[:, HALF:]
            back = mm_nt(moved[b, s, TGT, rows, :], w_down[...])
            sg = jax.nn.sigmoid(gate_pre)
            act = gate_pre * sg
            hid[s, rows, :] = (act * up_pre).astype(BF)
            cots[s, rows, :HALF] = (back * up_pre * sg * (1.0 + gate_pre * (1.0 - sg))).astype(BF)
            cots[s, rows, HALF:] = (back * act).astype(BF)
        grad_gu = mm_tn(moved[b, s, KEY, all_rows, :], cots[s, all_rows, :]).reshape(size_z, rows_gu, 256)
        grad_down = mm_tn(hid[s, all_rows, :], moved[b, s, TGT, all_rows, :]).reshape(size_z, rows_down, 256)
        if not opens:
            grad_gu = sums[:, :rows_gu, :] + grad_gu
            grad_down = sums[:, rows_gu:, :] + grad_down
        sums[:, :rows_gu, :] = grad_gu
        sums[:, rows_gu:, :] = grad_down
        if closes:
            ring_src[b, :, :rows_gu, :] = grad_gu.astype(BF)
            ring_src[b, :, rows_gu:, :] = grad_down.astype(BF)

    def send_ring(b):
        for k in peers:
            remote(
                ring_src.at[b, (z + k) & (size_z - 1)], ring_dst.at[b, k - 1],
                ring_s.at[b], ring_r.at[b], chip(k, k),
            ).start()

    def ring_all(b):
        return remote(ring_dst.at[b], ring_dst.at[b], ring_s.at[b], ring_r.at[b], twin)

    def send_all(b):
        total = sums[z]
        for k in peers:
            total = total + ring_dst[b, k - 1].astype(F32)
        full[b, core, z] = total.astype(BF)
        for k in peers:
            all_piece(b, z, k).start()
        twin_piece(b, z).start()

    def all_piece(b, at, k):
        return remote(full.at[b, core, at], full.at[b, core, at], all_s.at[b], all_r.at[b, k], chip(k, k))

    def all_all(b):
        return remote(ring_dst.at[b], ring_dst.at[b], all_s.at[b], all_r.at[b, 0], twin)

    def twin_piece(b, at):
        return remote(full.at[b, core, at], full.at[b, core, at], twin_s.at[b], twin_r.at[b], twin)

    def twin_copy(b):
        return remote(full.at[b, core], full.at[b, core], twin_s.at[b], twin_r.at[b], twin)

    def send_twin(b):
        for k in reversed(peers):
            at = (z - k) & (size_z - 1)
            all_piece(b, at, k).wait_recv()
            twin_piece(b, at).start()

    def set_weights(m, new):
        wide = new.astype(BF)
        weights_bf[m] = wide
        first = core == 0
        if m == 1:
            w_down[...] = jnp.where(first, new[:HALF, :], new[HALF:, :]).astype(BF)
        else:
            cols = slice(0, HALF) if m == 0 else slice(HALF, 256)
            w_gu[:, cols] = jnp.where(first, new[:, :HALF], new[:, HALF:]).astype(BF)

    def load_weights():
        w_load.wait()
        for m in range(3):
            set_weights(m, weights[m])

    def update(b):
        sides = [full[b, c, :, :rows_gu, :].reshape(256, 256) for c in range(2)]
        xs = [
            jnp.concatenate([side[:, :HALF] for side in sides], axis=1),
            jnp.concatenate([full[b, c, :, rows_gu:, :].reshape(HALF, 256) for c in range(2)], axis=0),
            jnp.concatenate([side[:, HALF:] for side in sides], axis=1),
        ]
        inverse = []
        for m in range(3):
            xf = xs[m].astype(F32)
            inverse.append(lax.rsqrt(jnp.sum(xf * xf, keepdims=True) + 1e-06))
        for step in range(NS_STEPS):
            grams = []
            for m in range(3):
                gram = mm_nt(xs[m], xs[m])
                if step == 0:
                    gram = gram * inverse[m] * inverse[m]
                grams.append(gram.astype(BF))
            polys = [
                (coef_b * grams[m].astype(F32) + coef_c * mm(grams[m], grams[m])).astype(BF) for m in range(3)
            ]
            for m in range(3):
                x = coef_a * xs[m].astype(F32) + mm(polys[m], xs[m])
                if step == 0:
                    x = x * inverse[m]
                xs[m] = x.astype(BF)
        for m in range(3):
            new = weights[m] - small_ref[3, pl.ds(own, 1), :][:, m : m + 1] * xs[m].astype(F32)
            weights[m] = new
            set_weights(m, new)

    def apply(b, chunks):
        for i in chunks:
            rows = slice(256 * i, 256 * i + 256)
            gate = mm(query[b, rows, :], weights_bf[0])
            up = mm(query[b, rows, :], weights_bf[2])
            mapped = mm((gate * jax.nn.sigmoid(gate) * up).astype(BF), weights_bf[1])
            squares = mapped * mapped
            high = squares.astype(BF)
            low = (squares - high.astype(F32)).astype(BF)
            ones = jnp.ones((8, 256), BF)
            row_src[b, i] = mm_nt(ones, high) + mm_nt(ones, low)
            if i == 0:
                map_dst[b, 0] = mapped.astype(BF)
            else:
                map_src[b, i - 1] = mapped.astype(BF)

    def send_rows(b):
        for dy, dz, r, t, row in ROUTES:
            remote(
                row_src.at[b, row // 256, :, pl.ds(row % 256, HALF)], row_dst.at[b, r - 1, :, pl.ds(t, HALF)],
                row_s.at[b], row_r.at[b], chip(-dy, -dz),
            ).start()

    def rows_all(b):
        return remote(row_dst.at[b], row_dst.at[b], row_s.at[b], row_r.at[b], twin)

    def send_back(b):
        for dy, dz, r, t, row in ROUTES:
            remote(
                map_src.at[b, row // 256 - 1, pl.ds(row % 256, HALF)], map_dst.at[b, r, pl.ds(t, HALF)],
                back_s.at[b], back_r.at[b], chip(-dy, -dz),
            ).start()

    def back_all(b):
        return remote(map_src.at[b], map_src.at[b], back_s.at[b], back_r.at[b], twin)

    def send_squares(b):
        sq_src[b] = row_src[b, 0] + row_dst[b, 0] + row_dst[b, 1] + row_dst[b, 2]
        for s in range(1, size_x):
            remote(sq_src.at[b], sq_dst.at[b, s - 1], sq_s.at[b], sq_r.at[b], across(s)).start()

    def squares_all(b):
        return remote(sq_dst.at[b], sq_dst.at[b], sq_s.at[b], sq_r.at[b], twin)

    def lay_out(b):
        for g in range(4):
            for r in range(4):
                for c in range(2):
                    for k in range(2):
                        t = 64 * g + 32 * k
                        tile_buf[g, 64 * r + 32 * c : 64 * r + 32 * c + 32, 128 * k : 128 * k + 128] = map_dst[
                            b, r, t : t + 32, 128 * c : 128 * c + 128
                        ]
            out = mm(scatter, tile_buf[g]).astype(BF)
            laid[b, 512 * g : 512 * g + 256, :] = out[:, :128]
            laid[b, 512 * g + 256 : 512 * g + 512, :] = out[:, 128:]

    def finish(b):
        total = sq_src[b]
        for s in range(1, size_x):
            total = total + sq_dst[b, s - 1]
        scale = lax.rsqrt(total * (1.0 / (total_heads * 256)) + 1e-06)
        scale = jnp.transpose(jnp.broadcast_to(scale[0:1, :], (128, 256)))
        gain = jnp.concatenate([small_ref[2, :, :128], small_ref[2, :, 128:]], axis=0)
        out = laid[b].astype(F32).reshape(256, 8, 128) * scale[:, None, :] * gain[None, :, :]
        out_ref[b] = out.reshape(2048, 128).astype(BF)

    sent = []

    def send(start, whole, b):
        start(b)
        sent.append(whole(b))

    def got(copy):
        copy.wait_recv()

    def first_gradients():
        sent.append(forward_all(0))
        for at in (1, 2, 3):
            pass_on(0, at)
        gradients(0, 0, opens=True)
        for at in range(4):
            passed(0, at)
        gradients(0, 1, closes=True)

    def later_tokens():
        for at in (1, 2, 3):
            pass_on(1, at)
        sent.append(forward_all(1))

    def later_queries():
        send(send_query, query_all, 0)
        send(send_query, query_all, 1)

    def send_mapped(b):
        send(send_rows, rows_all, b)
        send(send_back, back_all, b)

    steps = [
        lambda: split_heads(KEY, 0),
        lambda: pl.semaphore_wait(barrier, len(greeted)),
        lambda: send_kind(KEY, 0),
        lambda: split_heads(TGT, 0),
        lambda: send(lambda b: send_kind(TGT, b), moved_all, 0),
        lambda: send_own(0),
        signal_near,
        load_weights,
        lambda: split_heads(KEY, 1),
        lambda: split_heads(TGT, 1),
        signal_far,
        lambda: split_heads(QRY, 0),
        lambda: split_heads(QRY, 1),
        lambda: send_own(1),
        first_gradients,
        lambda: pl.semaphore_wait(far_sem, 2),
        lambda: send(send_ring, ring_all, 0),
        lambda: send(send_moved, moved_all, 1),
        lambda: got(ring_all(0)),
        lambda: send(send_all, all_all, 0),
        lambda: send(send_query, query_all, 0),
        later_tokens,
        lambda: send(send_twin, twin_copy, 0),
        lambda: send(send_query, query_all, 1),
        lambda: got(twin_copy(0)),
        lambda: update(0),
        lambda: [passed(1, at) for at in range(4)],
        lambda: gradients(1, 0, opens=True),
        lambda: gradients(1, 1, closes=True),
        lambda: send(send_ring, ring_all, 1),
        lambda: got(query_all(0)),
        lambda: apply(0, range(4)),
        lambda: got(ring_all(1)),
        lambda: send(send_all, all_all, 1),
        lambda: send_twin(1),
        lambda: sent.append(twin_copy(1)),
        lambda: send_mapped(0),
        lambda: got(twin_copy(1)),
        lambda: update(1),
        lambda: got(query_all(1)),
        lambda: apply(1, (3, 1, 2)),
        lambda: send_mapped(1),
        lambda: apply(1, (0,)),
        lambda: got(rows_all(0)),
        lambda: send(send_squares, squares_all, 0),
        lambda: got(back_all(0)),
        lambda: lay_out(0),
        lambda: got(rows_all(1)),
        lambda: send(send_squares, squares_all, 1),
        lambda: got(squares_all(0)),
        lambda: finish(0),
        lambda: got(back_all(1)),
        lambda: lay_out(1),
        lambda: got(squares_all(1)),
        lambda: finish(1),
    ]
    for step in steps:
        step()
    for copy in sent:
        copy.wait_send()


def per_device(size_z, size_x, queries, key_input, value_input, token_rates, fast_weights, update_rate, out_gain):
    piece = 384 // size_z

    def flat(a):
        return a.reshape(2, 256, 4, 2, 128).transpose(0, 1, 3, 2, 4).reshape(2, 2048, 128)

    small = (
        lax.pad(token_rates, 0.0, ((0, 2, 0), (0, 0, 0), (0, 0, 0)))
        + lax.pad(out_gain[None], 0.0, ((2, 1, 0), (0, 0, 0), (0, 0, 0)))
        + lax.pad(update_rate[None], 0.0, ((3, 0, 0), (0, 0, 0), (0, 253, 0)))
    )
    hbm = pl.BlockSpec(memory_space=pltpu.HBM)
    dma = pltpu.SemaphoreType.DMA
    out = pl.pallas_call(
        functools.partial(kernel, size_z, size_x),
        out_shape=jax.ShapeDtypeStruct((2, 2048, 128), BF),
        in_specs=[hbm] * 4 + [pl.BlockSpec(memory_space=pltpu.VMEM)],
        out_specs=pl.BlockSpec(memory_space=pltpu.VMEM),
        scratch_shapes=[
            pltpu.VMEM((3, 2, 2048, 128), BF),
            pltpu.VMEM((2, 2048, 128), BF),
            pltpu.VMEM((2, 2, 2, 1024, 256), BF),
            pltpu.VMEM((2, 2, 3, 256, 256), BF),
            pltpu.VMEM((2, 1024, 256), BF),
            pltpu.VMEM((2, 3, 256, 256), BF),
            pltpu.VMEM((3, 256, 256), F32),
            pltpu.VMEM((3, 256, 256), BF),
            pltpu.VMEM((256, 256), BF),
            pltpu.VMEM((128, 256), BF),
            pltpu.VMEM((2, 1024, 128), BF),
            pltpu.VMEM((2, 1024, 256), BF),
            pltpu.VMEM((size_z, piece, 256), F32),
            pltpu.VMEM((2, size_z, piece, 256), BF),
            pltpu.VMEM((2, size_z - 1, piece, 256), BF),
            pltpu.VMEM((2, 2, size_z, piece, 256), BF),
            pltpu.VMEM((2, 3, 256, 256), BF),
            pltpu.VMEM((2, 4, 256, 256), BF),
            pltpu.VMEM((4, 256, 256), BF),
            pltpu.VMEM((2, 4, 8, 256), F32),
            pltpu.VMEM((2, 3, 8, 256), F32),
            pltpu.VMEM((2, 8, 256), F32),
            pltpu.VMEM((2, max(size_x - 1, 1), 8, 256), F32),
            pltpu.SemaphoreType.REGULAR, pltpu.SemaphoreType.REGULAR,
            dma((3, 2)), dma,
            dma((2,)), dma((2, len(MOVES))), dma((2,)), dma((2, 4)),
            *[dma((2,)) for _ in range(5)], dma((2, size_z)), *[dma((2,)) for _ in range(8)],
        ],
        compiler_params=pltpu.CompilerParams(
            collective_id=0, has_side_effects=True, vmem_limit_bytes=53760 * 1024
        ),
        cost_estimate=pl.CostEstimate(flops=12_000_000_000, bytes_accessed=5_000_000, transcendentals=1_000_000),
    )(flat(queries), flat(key_input), flat(value_input), fast_weights, small)
    return out.reshape(2, 256, 2, 4, 128).transpose(0, 1, 3, 2, 4).reshape(2, 256, 4, 256)


def solution(mesh):
    size_z = mesh.shape["tok"] // (2 * SIZE_Y)
    return jax.shard_map(
        functools.partial(per_device, size_z, mesh.shape["head"]),
        mesh=mesh,
        in_specs=(
            P(None, "tok", "head", None),
            P(None, "tok", "head", None),
            P(None, "tok", "head", None),
            P(None, "head", "tok"),
            P("head", None, None, None),
            P("head", None),
            P("head", None),
        ),
        out_specs=P(None, "tok", "head", None),
        check_vma=False,
    )
```

```python
import functools

import jax
import jax.numpy as jnp
from jax import lax
from jax.experimental import pallas as pl
from jax.experimental.pallas import tpu as pltpu
from jax.sharding import PartitionSpec as P

NS_STEPS = 3
SIZE_Y = 4

coef_a = 3.4445
coef_b = -4.775
coef_c = 2.0315

BF = jnp.bfloat16
F32 = jnp.float32
MESH = pl.DeviceIdType.MESH
KEY, TGT, QRY = 0, 1, 2
HALF = 128

ROUTES = (
    (-1, 1, 2, 0, 768),
    (1, -1, 2, 128, 896),
    (0, 1, 1, 0, 256),
    (-1, 0, 1, 128, 384),
    (0, -1, 3, 0, 512),
    (1, 0, 3, 128, 640),
)
MOVES = (
    (-1, 1, 2, 0, 128, 768),
    (1, -1, 2, 128, 128, 896),
    (0, 1, 1, 0, 128, 256),
    (-1, 0, 1, 128, 128, 384),
    (0, -1, 3, 0, 128, 512),
    (1, 0, 3, 128, 128, 640),
)


def mm(a, b):
    return jnp.dot(a, b, preferred_element_type=F32)


def mm_nt(a, b):
    return lax.dot_general(a, b, (((1,), (1,)), ((), ())), preferred_element_type=F32)


def mm_tn(a, b):
    return lax.dot_general(a, b, (((0,), (0,)), ((), ())), preferred_element_type=F32)


def kernel(
    size_z, size_x,
    q_hbm, k_hbm, v_hbm, w_hbm, small_ref, out_ref,
    raw, laid, moved, staged, query, query_staged,
    weights, weights_bf, w_gu, w_down, hid, cots, sums, ring_src, ring_dst, full,
    map_src, map_dst, tile_buf, row_src, row_dst, sq_src, sq_dst,
    near_sem, far_sem, load_sem, w_sem, move_s, move_r, fwd_s, fwd_r, query_s, query_r,
    ring_s, ring_r, all_s, all_r, twin_s, twin_r, row_s, row_r, back_s, back_r, sq_s, sq_r,
):
    bits_z = size_z.bit_length() - 1
    rows_gu, rows_down = 256 // size_z, 128 // size_z
    total_heads = 4 * size_x
    tok = lax.axis_index("tok")
    head_x = lax.axis_index("head")
    core = tok & 1
    z = (tok >> 1) & (size_z - 1)
    y = tok >> (1 + bits_z)
    own = (z - y) & 3

    def chip(dy, dz, dc=0):
        at_y = (y + dy) & (SIZE_Y - 1)
        at_z = (z + dz) & (size_z - 1)
        return {"tok": (at_y * size_z + at_z) * 2 + (core ^ dc)}

    def across(step):
        return {"head": (head_x + step) & (size_x - 1)}

    peers = sorted(range(1, size_z), key=lambda k: abs(k - size_z // 2))

    sources = {KEY: k_hbm, TGT: v_hbm, QRY: q_hbm}

    def load(kind, b):
        return pltpu.make_async_copy(sources[kind].at[b], raw.at[kind, b], load_sem.at[kind, b])

    barrier = pltpu.get_barrier_semaphore()
    near = [chip(dy, dz) for dy, dz, *_ in ROUTES]
    greeted = [*near]
    greeted += [across(s) for s in range(1, size_x)]
    greeted += [chip(0, 0, 1)]
    load(KEY, 0).start()
    load(TGT, 0).start()
    for device in greeted:
        pl.semaphore_signal(barrier, inc=1, device_id=device, device_id_type=MESH)
    w_load = pltpu.make_async_copy(w_hbm.at[own], weights, w_sem)
    w_load.start()
    for kind, b in ((KEY, 1), (TGT, 1), (QRY, 0), (QRY, 1)):
        load(kind, b).start()

    def signal_near():
        for device in near:
            pl.semaphore_signal(near_sem, inc=1, device_id=device, device_id_type=MESH)

    def signal_far():
        pl.semaphore_wait(near_sem, len(near))
        for dz in (2, -2):
            pl.semaphore_signal(far_sem, inc=1, device_id=chip(0, dz), device_id_type=MESH)

    rows_i = lax.broadcasted_iota(jnp.int32, (256, 256), 0)
    cols_i = lax.broadcasted_iota(jnp.int32, (256, 256), 1)

    def source_row(i):
        return (i & 31) * 8 + ((i >> 5) & 1) * 4 + (((i >> 6) + own) & 3)

    gather = jnp.where(source_row(rows_i) == cols_i, 1.0, 0.0).astype(BF)
    scatter = jnp.where(source_row(cols_i) == rows_i, 1.0, 0.0).astype(BF)

    def split_heads(kind, b):
        load(kind, b).wait()
        if kind == TGT:
            rates = []
            for r in range(4):
                row = small_ref[b, pl.ds((r + own) & 3, 1), :]
                rates.append(-jnp.transpose(jnp.broadcast_to(row, (128, 256))))
        for g in range(4):
            lo = raw[kind, b, 512 * g : 512 * g + 256, :]
            hi = raw[kind, b, 512 * g + 256 : 512 * g + 512, :]
            out = mm(gather, jnp.concatenate([lo, hi], axis=1))
            for r in range(4):
                for c in range(2):
                    for k in range(2):
                        t = 64 * g + 32 * k
                        tile = out[64 * r + 32 * c : 64 * r + 32 * c + 32, 128 * k : 128 * k + 128]
                        if kind == TGT:
                            tile = tile * rates[r][t : t + 32, :]
                        tile = tile.astype(BF)
                        cols = slice(128 * c, 128 * c + 128)
                        if kind == QRY and r == 0:
                            query[b, t : t + 32, cols] = tile
                        elif kind == QRY:
                            query_staged[b, r - 1, t : t + 32, cols] = tile
                        elif r == 0:
                            moved[b, 0, kind, t : t + 32, cols] = tile
                        else:
                            staged[b, kind, r - 1, t : t + 32, cols] = tile

    def remote(src, dst, s, r, device):
        return pltpu.make_async_remote_copy(
            src_ref=src, dst_ref=dst, send_sem=s, recv_sem=r, device_id=device, device_id_type=MESH
        )

    twin = chip(0, 0, 1)

    def moved_piece(b, i):
        dy, dz, r, t, n, row = MOVES[i]
        return remote(
            staged.at[b, :, r - 1, pl.ds(t, n)],
            moved.at[b, 0, :, pl.ds(row, n)],
            move_s.at[b], move_r.at[b, i], chip(dy, dz),
        )

    def send_kind(kind, b):
        for i, (dy, dz, r, t, n, row) in enumerate(MOVES):
            remote(
                staged.at[b, kind, r - 1, pl.ds(t, n)],
                moved.at[b, 0, kind, pl.ds(row, n)],
                move_s.at[b], move_r.at[b, i], chip(dy, dz),
            ).start()

    def send_moved(b):
        send_kind(KEY, b)
        send_kind(TGT, b)

    def moved_all(b):
        return remote(staged.at[b], staged.at[b], move_s.at[b], move_r.at[b, 0], twin)

    def forward_rows(b, at, row, n):
        rows = pl.ds(row, n)
        return remote(moved.at[b, 0, :, rows], moved.at[b, 1, :, rows], fwd_s.at[b], fwd_r.at[b, at], twin)

    def send_own(b):
        forward_rows(b, 0, 0, 256).start()

    def pass_on(b, at):
        for i, (*_, n, row) in enumerate(MOVES):
            if row // 256 == at:
                moved_piece(b, i).wait_recv()
                forward_rows(b, at, row, n).start()

    def passed(b, at):
        forward_rows(b, at, 256 * at, 256).wait_recv()

    def forward_all(b):
        return remote(moved.at[b, 0], moved.at[b, 1], fwd_s.at[b], fwd_r.at[b, 0], twin)

    def send_query(b):
        for dy, dz, r, t, row in ROUTES:
            remote(
                query_staged.at[b, r - 1, pl.ds(t, HALF)], query.at[b, pl.ds(row, HALF)],
                query_s.at[b], query_r.at[b], chip(dy, dz),
            ).start()

    def query_all(b):
        return remote(query_staged.at[b], query_staged.at[b], query_s.at[b], query_r.at[b], twin)

    def gradients(b, s, chunks=range(4), opens=False, closes=False):
        all_rows = slice(256 * chunks[0], 256 * chunks[-1] + 256)
        for i in chunks:
            rows = slice(256 * i, 256 * i + 256)
            pre = mm(moved[b, s, KEY, rows, :], w_gu[...])
            gate_pre, up_pre = pre[:, :HALF], pre[:, HALF:]
            back = mm_nt(moved[b, s, TGT, rows, :], w_down[...])
            sg = jax.nn.sigmoid(gate_pre)
            act = gate_pre * sg
            hid[s, rows, :] = (act * up_pre).astype(BF)
            cots[s, rows, :HALF] = (back * up_pre * sg * (1.0 + gate_pre * (1.0 - sg))).astype(BF)
            cots[s, rows, HALF:] = (back * act).astype(BF)
        grad_gu = mm_tn(moved[b, s, KEY, all_rows, :], cots[s, all_rows, :]).reshape(size_z, rows_gu, 256)
        grad_down = mm_tn(hid[s, all_rows, :], moved[b, s, TGT, all_rows, :]).reshape(size_z, rows_down, 256)
        if not opens:
            grad_gu = sums[:, :rows_gu, :] + grad_gu
            grad_down = sums[:, rows_gu:, :] + grad_down
        sums[:, :rows_gu, :] = grad_gu
        sums[:, rows_gu:, :] = grad_down
        if closes:
            ring_src[b, :, :rows_gu, :] = grad_gu.astype(BF)
            ring_src[b, :, rows_gu:, :] = grad_down.astype(BF)

    def turned(k):
        return k + core * (size_z - 2 * k)

    def send_ring(b):
        for k in map(turned, peers):
            remote(
                ring_src.at[b, (z + k) & (size_z - 1)], ring_dst.at[b, k - 1],
                ring_s.at[b], ring_r.at[b], chip(k, k),
            ).start()

    def ring_all(b):
        return remote(ring_dst.at[b], ring_dst.at[b], ring_s.at[b], ring_r.at[b], twin)

    def send_all(b):
        total = sums[z]
        for k in peers:
            total = total + ring_dst[b, k - 1].astype(F32)
        full[b, core, z] = total.astype(BF)
        for k in map(turned, peers):
            all_piece(b, z, k).start()
        twin_piece(b, z).start()

    def all_piece(b, at, k):
        return remote(full.at[b, core, at], full.at[b, core, at], all_s.at[b], all_r.at[b, k], chip(k, k))

    def all_all(b):
        return remote(ring_dst.at[b], ring_dst.at[b], all_s.at[b], all_r.at[b, 0], twin)

    def twin_piece(b, at):
        return remote(full.at[b, core, at], full.at[b, core, at], twin_s.at[b], twin_r.at[b], twin)

    def twin_copy(b):
        return remote(full.at[b, core], full.at[b, core], twin_s.at[b], twin_r.at[b], twin)

    def send_twin(b):
        for k in reversed(peers):
            at = (z - k) & (size_z - 1)
            all_piece(b, at, k).wait_recv()
            twin_piece(b, at).start()

    def set_weights(m, new):
        wide = new.astype(BF)
        weights_bf[m] = wide
        first = core == 0
        if m == 1:
            w_down[...] = jnp.where(first, new[:HALF, :], new[HALF:, :]).astype(BF)
        else:
            cols = slice(0, HALF) if m == 0 else slice(HALF, 256)
            w_gu[:, cols] = jnp.where(first, new[:, :HALF], new[:, HALF:]).astype(BF)

    def load_weights():
        w_load.wait()
        for m in range(3):
            set_weights(m, weights[m])

    def update(b):
        sides = [full[b, c, :, :rows_gu, :].reshape(256, 256) for c in range(2)]
        xs = [
            jnp.concatenate([side[:, :HALF] for side in sides], axis=1),
            jnp.concatenate([full[b, c, :, rows_gu:, :].reshape(HALF, 256) for c in range(2)], axis=0),
            jnp.concatenate([side[:, HALF:] for side in sides], axis=1),
        ]
        inverse = []
        for m in range(3):
            xf = xs[m].astype(F32)
            inverse.append(lax.rsqrt(jnp.sum(xf * xf, keepdims=True) + 1e-06))
        for step in range(NS_STEPS):
            grams = []
            for m in range(3):
                gram = mm_nt(xs[m], xs[m])
                if step == 0:
                    gram = gram * inverse[m] * inverse[m]
                grams.append(gram.astype(BF))
            polys = [
                (coef_b * grams[m].astype(F32) + coef_c * mm(grams[m], grams[m])).astype(BF) for m in range(3)
            ]
            for m in range(3):
                x = coef_a * xs[m].astype(F32) + mm(polys[m], xs[m])
                if step == 0:
                    x = x * inverse[m]
                xs[m] = x.astype(BF)
        for m in range(3):
            new = weights[m] - small_ref[3, pl.ds(own, 1), :][:, m : m + 1] * xs[m].astype(F32)
            weights[m] = new
            set_weights(m, new)

    def apply(b, chunks):
        for i in chunks:
            rows = slice(256 * i, 256 * i + 256)
            gate = mm(query[b, rows, :], weights_bf[0])
            up = mm(query[b, rows, :], weights_bf[2])
            mapped = mm((gate * jax.nn.sigmoid(gate) * up).astype(BF), weights_bf[1])
            squares = mapped * mapped
            high = squares.astype(BF)
            low = (squares - high.astype(F32)).astype(BF)
            ones = jnp.ones((8, 256), BF)
            row_src[b, i] = mm_nt(ones, high) + mm_nt(ones, low)
            if i == 0:
                map_dst[b, 0] = mapped.astype(BF)
            else:
                map_src[b, i - 1] = mapped.astype(BF)

    def send_rows(b):
        for dy, dz, r, t, row in ROUTES:
            remote(
                row_src.at[b, row // 256, :, pl.ds(row % 256, HALF)], row_dst.at[b, r - 1, :, pl.ds(t, HALF)],
                row_s.at[b], row_r.at[b], chip(-dy, -dz),
            ).start()

    def rows_all(b):
        return remote(row_dst.at[b], row_dst.at[b], row_s.at[b], row_r.at[b], twin)

    def send_back(b):
        for dy, dz, r, t, row in ROUTES:
            remote(
                map_src.at[b, row // 256 - 1, pl.ds(row % 256, HALF)], map_dst.at[b, r, pl.ds(t, HALF)],
                back_s.at[b], back_r.at[b], chip(-dy, -dz),
            ).start()

    def back_all(b):
        return remote(map_src.at[b], map_src.at[b], back_s.at[b], back_r.at[b], twin)

    def send_squares(b):
        sq_src[b] = row_src[b, 0] + row_dst[b, 0] + row_dst[b, 1] + row_dst[b, 2]
        for s in range(1, size_x):
            remote(sq_src.at[b], sq_dst.at[b, s - 1], sq_s.at[b], sq_r.at[b], across(s)).start()

    def squares_all(b):
        return remote(sq_dst.at[b], sq_dst.at[b], sq_s.at[b], sq_r.at[b], twin)

    def lay_out(b):
        for g in range(4):
            for r in range(4):
                for c in range(2):
                    for k in range(2):
                        t = 64 * g + 32 * k
                        tile_buf[g, 64 * r + 32 * c : 64 * r + 32 * c + 32, 128 * k : 128 * k + 128] = map_dst[
                            b, r, t : t + 32, 128 * c : 128 * c + 128
                        ]
            out = mm(scatter, tile_buf[g]).astype(BF)
            laid[b, 512 * g : 512 * g + 256, :] = out[:, :128]
            laid[b, 512 * g + 256 : 512 * g + 512, :] = out[:, 128:]

    def finish(b):
        total = sq_src[b]
        for s in range(1, size_x):
            total = total + sq_dst[b, s - 1]
        scale = lax.rsqrt(total * (1.0 / (total_heads * 256)) + 1e-06)
        scale = jnp.transpose(jnp.broadcast_to(scale[0:1, :], (128, 256)))
        gain = jnp.concatenate([small_ref[2, :, :128], small_ref[2, :, 128:]], axis=0)
        out = laid[b].astype(F32).reshape(256, 8, 128) * scale[:, None, :] * gain[None, :, :]
        out_ref[b] = out.reshape(2048, 128).astype(BF)

    sent = []

    def send(start, whole, b):
        start(b)
        sent.append(whole(b))

    def got(copy):
        copy.wait_recv()

    def first_gradients():
        sent.append(forward_all(0))
        for at in (1, 2, 3):
            pass_on(0, at)
        gradients(0, 0, opens=True)
        for at in range(4):
            passed(0, at)
        gradients(0, 1, closes=True)

    def later_tokens():
        for at in (1, 2, 3):
            pass_on(1, at)
        sent.append(forward_all(1))

    def later_queries():
        send(send_query, query_all, 0)
        send(send_query, query_all, 1)

    def send_mapped(b):
        send(send_rows, rows_all, b)
        send(send_back, back_all, b)

    steps = [
        lambda: split_heads(KEY, 0),
        lambda: pl.semaphore_wait(barrier, len(greeted)),
        lambda: send_kind(KEY, 0),
        lambda: split_heads(TGT, 0),
        lambda: send(lambda b: send_kind(TGT, b), moved_all, 0),
        lambda: send_own(0),
        signal_near,
        load_weights,
        lambda: split_heads(KEY, 1),
        lambda: split_heads(TGT, 1),
        signal_far,
        lambda: split_heads(QRY, 0),
        lambda: split_heads(QRY, 1),
        lambda: send_own(1),
        first_gradients,
        lambda: pl.semaphore_wait(far_sem, 2),
        lambda: send(send_ring, ring_all, 0),
        lambda: send(send_moved, moved_all, 1),
        lambda: got(ring_all(0)),
        lambda: send(send_all, all_all, 0),
        lambda: send(send_query, query_all, 0),
        later_tokens,
        lambda: send(send_twin, twin_copy, 0),
        lambda: send(send_query, query_all, 1),
        lambda: got(twin_copy(0)),
        lambda: update(0),
        lambda: [passed(1, at) for at in range(4)],
        lambda: gradients(1, 0, opens=True),
        lambda: gradients(1, 1, closes=True),
        lambda: send(send_ring, ring_all, 1),
        lambda: got(query_all(0)),
        lambda: apply(0, range(4)),
        lambda: got(ring_all(1)),
        lambda: send(send_all, all_all, 1),
        lambda: send_twin(1),
        lambda: sent.append(twin_copy(1)),
        lambda: send_mapped(0),
        lambda: got(twin_copy(1)),
        lambda: update(1),
        lambda: got(query_all(1)),
        lambda: apply(1, (3, 1, 2)),
        lambda: send_mapped(1),
        lambda: apply(1, (0,)),
        lambda: got(rows_all(0)),
        lambda: send(send_squares, squares_all, 0),
        lambda: got(back_all(0)),
        lambda: lay_out(0),
        lambda: got(rows_all(1)),
        lambda: send(send_squares, squares_all, 1),
        lambda: got(squares_all(0)),
        lambda: finish(0),
        lambda: got(back_all(1)),
        lambda: lay_out(1),
        lambda: got(squares_all(1)),
        lambda: finish(1),
    ]
    for step in steps:
        step()
    for copy in sent:
        copy.wait_send()


def per_device(size_z, size_x, queries, key_input, value_input, token_rates, fast_weights, update_rate, out_gain):
    piece = 384 // size_z

    def flat(a):
        return a.reshape(2, 256, 4, 2, 128).transpose(0, 1, 3, 2, 4).reshape(2, 2048, 128)

    small = (
        lax.pad(token_rates, 0.0, ((0, 2, 0), (0, 0, 0), (0, 0, 0)))
        + lax.pad(out_gain[None], 0.0, ((2, 1, 0), (0, 0, 0), (0, 0, 0)))
        + lax.pad(update_rate[None], 0.0, ((3, 0, 0), (0, 0, 0), (0, 253, 0)))
    )
    hbm = pl.BlockSpec(memory_space=pltpu.HBM)
    dma = pltpu.SemaphoreType.DMA
    out = pl.pallas_call(
        functools.partial(kernel, size_z, size_x),
        out_shape=jax.ShapeDtypeStruct((2, 2048, 128), BF),
        in_specs=[hbm] * 4 + [pl.BlockSpec(memory_space=pltpu.VMEM)],
        out_specs=pl.BlockSpec(memory_space=pltpu.VMEM),
        scratch_shapes=[
            pltpu.VMEM((3, 2, 2048, 128), BF),
            pltpu.VMEM((2, 2048, 128), BF),
            pltpu.VMEM((2, 2, 2, 1024, 256), BF),
            pltpu.VMEM((2, 2, 3, 256, 256), BF),
            pltpu.VMEM((2, 1024, 256), BF),
            pltpu.VMEM((2, 3, 256, 256), BF),
            pltpu.VMEM((3, 256, 256), F32),
            pltpu.VMEM((3, 256, 256), BF),
            pltpu.VMEM((256, 256), BF),
            pltpu.VMEM((128, 256), BF),
            pltpu.VMEM((2, 1024, 128), BF),
            pltpu.VMEM((2, 1024, 256), BF),
            pltpu.VMEM((size_z, piece, 256), F32),
            pltpu.VMEM((2, size_z, piece, 256), BF),
            pltpu.VMEM((2, size_z - 1, piece, 256), BF),
            pltpu.VMEM((2, 2, size_z, piece, 256), BF),
            pltpu.VMEM((2, 3, 256, 256), BF),
            pltpu.VMEM((2, 4, 256, 256), BF),
            pltpu.VMEM((4, 256, 256), BF),
            pltpu.VMEM((2, 4, 8, 256), F32),
            pltpu.VMEM((2, 3, 8, 256), F32),
            pltpu.VMEM((2, 8, 256), F32),
            pltpu.VMEM((2, max(size_x - 1, 1), 8, 256), F32),
            pltpu.SemaphoreType.REGULAR, pltpu.SemaphoreType.REGULAR,
            dma((3, 2)), dma,
            dma((2,)), dma((2, len(MOVES))), dma((2,)), dma((2, 4)),
            *[dma((2,)) for _ in range(5)], dma((2, size_z)), *[dma((2,)) for _ in range(8)],
        ],
        compiler_params=pltpu.CompilerParams(
            collective_id=0, has_side_effects=True, vmem_limit_bytes=53760 * 1024
        ),
        cost_estimate=pl.CostEstimate(flops=12_000_000_000, bytes_accessed=5_000_000, transcendentals=1_000_000),
    )(flat(queries), flat(key_input), flat(value_input), fast_weights, small)
    return out.reshape(2, 256, 2, 4, 128).transpose(0, 1, 3, 2, 4).reshape(2, 256, 4, 256)


def solution(mesh):
    size_z = mesh.shape["tok"] // (2 * SIZE_Y)
    return jax.shard_map(
        functools.partial(per_device, size_z, mesh.shape["head"]),
        mesh=mesh,
        in_specs=(
            P(None, "tok", "head", None),
            P(None, "tok", "head", None),
            P(None, "tok", "head", None),
            P(None, "head", "tok"),
            P("head", None, None, None),
            P("head", None),
            P("head", None),
        ),
        out_specs=P(None, "tok", "head", None),
        check_vma=False,
    )
```
